32 devices in a mesh: dp: 4 (over x, core), ctx: 8 (over z, y).
Axes of the slice: x: 2, y: 2, z: 4, core: 2. Of those that a mesh axis runs over, the one named last changes fastest.
Arguments:
- tokens: bfloat16 [4096, 4096], P(('dp', 'ctx')), parts along dimension 0, may hold values from -6 to 6
- pick_flags: int32 [4096], P(('dp', 'ctx')), parts along dimension 0, may hold values from 0 to 1, as said below
- gate_scales: bfloat16 [4096], P(('dp', 'ctx')), parts along dimension 0, may hold values from 0.099609375 to 1
- attn_gain: float32 [4096], replicated, may hold values from 0.4 to 1.6
- query_weight: bfloat16 [4096, 4096], P(None, 'ctx')
- key_weight: bfloat16 [4096, 1024], P(None, 'ctx')
- value_matrix: bfloat16 [4096, 1024], P(None, 'ctx'), may hold values from -0.09375 to 0.09375
- output_weight: bfloat16 [4096, 4096], P('ctx'), may hold values from -0.09375 to 0.09375
- ffn_gain: float32 [4096], replicated, may hold values from 0.25 to 1.75
- gate_weight: bfloat16 [4096, 11264], P(None, 'ctx'), may hold values from -0.09375 to 0.09375
- up_weight: bfloat16 [4096, 11264], P(None, 'ctx'), may hold values from -0.09375 to 0.09375
- down_weight: bfloat16 [11264, 4096], P('ctx'), may hold values from -0.0546875 to 0.0546875
Outputs:
- block_out: bfloat16 [4096, 4096], P(('dp', 'ctx')), parts along dimension 0
The draws below stay inside these ranges and needn't reach their ends.
There are 4 independent parts, one for each index of `dp`. The reference program is written for one: setup_inputs(seed, part) draws one part's arguments, and reference() takes and returns one part's arrays. A program takes and returns all parts, laid end to end along the dimension named above; an argument that names none is the same for every part. Nothing has to cross between parts.
Inputs may be any that keep to these rules, and one draw needn't show every extreme that they name: `pick_flags`: each device's 128 tokens hold at most 32 picks, the first device exactly 32; each document holds exactly 128 picks; a device may hold none.
All inputs are finite; a program needn't handle non-finite values.
Results may differ from the reference program's by a relative error of at most 0.01.
Values may be sent and summed in bfloat16 or wider, within the bound.
No kernel may reach another device: no remote copies, remote signals or barrier semaphores. Data moves between devices by JAX's collectives and lax.ppermute only.
A program may use at most 128 MiB of HBM per device.

```python
import jax
import jax.numpy as jnp
from jax import lax

MODEL_WIDTH = 4096
QUERY_HEADS = 32
KEY_VALUE_HEADS = 8
HEAD_SIZE = 128
FF = 11264
TOK_DEV = 128
PICK_DEV = 16
MOST = 32
PICKED_TOKENS = 128
TOKENS = 1024
N_CTX = 8


def draw_pick_flags(key, part):
    counts = jnp.full((N_CTX,), PICK_DEV, jnp.int32)
    others = 1 + jax.random.permutation(jax.random.fold_in(key, 1), N_CTX - 1)
    counts = counts.at[0].set(MOST).at[others[0]].set(0)
    remain = others[1:]
    for mixing in range(3):
        shuffled = jax.random.permutation(jax.random.fold_in(key, 10 + mixing), remain)
        givers = shuffled[0::2]
        takers = shuffled[1::2]
        give_now = counts[givers]
        take_now = counts[takers]
        upper_bound = jnp.minimum(give_now, MOST - take_now)
        lower_bound = -jnp.minimum(take_now, MOST - give_now)
        amount = jax.random.randint(jax.random.fold_in(key, 20 + mixing), givers.shape, lower_bound, upper_bound + 1)
        counts = counts.at[givers].add(-amount).at[takers].add(amount)
    device_keys = jax.random.split(jax.random.fold_in(key, 2), N_CTX)
    shuffled_ids = jax.vmap(lambda single: jax.random.permutation(single, TOK_DEV))(device_keys)
    picked = (shuffled_ids < counts[:, None]).astype(jnp.int32)
    return picked.reshape(TOK_DEV * N_CTX)


def repeated_keys(key):
    return jax.random.normal(jax.random.fold_in(key, 71), (MODEL_WIDTH, HEAD_SIZE * KEY_VALUE_HEADS), jnp.float32) * MODEL_WIDTH ** (-0.5)


def draw_key_weight(key, part):
    return repeated_keys(key).astype(jnp.bfloat16)


def draw_query_weight(key, part):
    noise = jax.random.normal(jax.random.fold_in(key, 72), (MODEL_WIDTH, QUERY_HEADS * HEAD_SIZE), jnp.float32) * MODEL_WIDTH ** (-0.5)
    return noise.astype(jnp.bfloat16)


def levels(stream_key, dims, shards, least, top_value):
    loudness, own = 1.0, jax.random.fold_in(stream_key, 6)
    for axis_at, parts in shards:
        steps = jnp.exp(jax.random.uniform(jax.random.fold_in(own, axis_at), (parts,), jnp.float32, least / len(shards), top_value / len(shards)))
        loudness = loudness * jnp.repeat(steps, dims[axis_at] // parts).reshape([-1 if axis == axis_at else 1 for axis in range(len(dims))])
    return loudness


def centred(stream_key, dims, deviation, reach, pieces=(), kind=jnp.bfloat16):
    level = levels(stream_key, dims, pieces, -0.22, 0.18) if pieces else 1.0
    result = jax.random.normal(stream_key, dims, jnp.float32) * deviation * level
    return jnp.minimum(jnp.maximum(result, -reach), reach).astype(kind)


def setup_inputs(seed: int = 0, part: int = 0) -> dict:
    splits = jax.random.split(jax.random.key(seed), 13)
    part_keys = jax.random.split(jax.random.fold_in(splits[12], part), 13)
    return {
        "tokens": centred(part_keys[0], (TOKENS, MODEL_WIDTH), 1.0, 6.0, ((0, 8),)),
        "pick_flags": draw_pick_flags(jax.random.fold_in(jax.random.fold_in(splits[12], part), 71), part),
        "gate_scales": jnp.clip(0.099609375 + 0.9003906 * jax.random.uniform(part_keys[2], (TOKENS,), jnp.float32) ** levels(part_keys[2], (TOKENS,), ((0, 8),), -0.2, 0.2), 0.099609375, 1.0).astype(jnp.bfloat16),
        "attn_gain": jnp.clip(jax.random.uniform(splits[3], (MODEL_WIDTH,), jnp.float32, 0.4, 1.6), 0.4, 1.6),
        "query_weight": draw_query_weight(jax.random.fold_in(splits[12], 71), part),
        "key_weight": draw_key_weight(jax.random.fold_in(splits[12], 71), part),
        "value_matrix": centred(splits[6], (MODEL_WIDTH, HEAD_SIZE * KEY_VALUE_HEADS), MODEL_WIDTH ** -0.5, 0.09375, ((1, 8),)),
        "output_weight": centred(splits[7], (QUERY_HEADS * HEAD_SIZE, MODEL_WIDTH), (QUERY_HEADS * HEAD_SIZE) ** -0.5, 0.09375, ((0, 8),)),
        "ffn_gain": jnp.clip(1.0 + 0.15 * jax.random.normal(splits[8], (MODEL_WIDTH,), jnp.float32), 0.25, 1.75),
        "gate_weight": centred(splits[9], (MODEL_WIDTH, FF), MODEL_WIDTH ** -0.5, 0.09375, ((1, 8),)),
        "up_weight": centred(splits[10], (MODEL_WIDTH, FF), MODEL_WIDTH ** -0.5, 0.09375, ((1, 8),)),
        "down_weight": centred(splits[11], (FF, MODEL_WIDTH), FF ** -0.5, 0.0546875, ((0, 8),)),
    }


norm_eps = 1e-05
rope_base = 500000.0

def rms_scale(matrix, gain_vec):
    mean_square = lax.optimization_barrier(jnp.mean(matrix * matrix, axis=-1, keepdims=True))
    return matrix * lax.rsqrt(mean_square + norm_eps) * gain_vec

def apply_rotary(values, token_positions):
    half_dim = values.shape[-1] // 2
    frequency = rope_base ** (-(jnp.arange(half_dim, dtype=jnp.float32) * 2.0) / values.shape[-1])
    angles = token_positions.astype(jnp.float32)[:, None] * frequency[None, :]
    cosine = jnp.cos(angles)[:, None, :]
    sine_part = jnp.sin(angles)[:, None, :]
    lower_half = values[..., :half_dim]
    upper_half = values[..., half_dim:]
    return jnp.concatenate((lower_half * cosine - upper_half * sine_part, upper_half * cosine + lower_half * sine_part), axis=-1)

def rounded(values):
    return lax.optimization_barrier(values.astype(jnp.bfloat16)).astype(jnp.float32)

def reference(tokens, pick_flags, gate_scales, attn_gain, query_weight, key_weight, value_matrix, output_weight, ffn_gain, gate_weight, up_weight, down_weight):
    picked_index = jnp.nonzero(pick_flags, size=PICKED_TOKENS)[0].astype(jnp.int32)
    picked_rows = tokens[picked_index]
    scales = gate_scales[picked_index].astype(jnp.float32)
    normalized_rows = rms_scale(picked_rows.astype(jnp.float32), attn_gain).astype(jnp.bfloat16)
    queries = jnp.dot(normalized_rows, query_weight, preferred_element_type=jnp.float32).reshape(PICKED_TOKENS, QUERY_HEADS, HEAD_SIZE)
    queries = apply_rotary(queries, picked_index).astype(jnp.bfloat16)
    unrotated_keys = jnp.dot(normalized_rows, key_weight, preferred_element_type=jnp.float32).astype(jnp.bfloat16)
    repeated_values = jnp.dot(normalized_rows, value_matrix, preferred_element_type=jnp.float32).astype(jnp.bfloat16)
    repeated_values = jnp.transpose(repeated_values.reshape(PICKED_TOKENS, HEAD_SIZE, KEY_VALUE_HEADS), (0, 2, 1))
    key_heads = jnp.transpose(unrotated_keys.astype(jnp.float32).reshape(PICKED_TOKENS, HEAD_SIZE, KEY_VALUE_HEADS), (0, 2, 1))
    rotated_keys = apply_rotary(key_heads, picked_index).astype(jnp.bfloat16)
    query_group_width = QUERY_HEADS // KEY_VALUE_HEADS
    allowed = picked_index[None, :] <= picked_index[:, None]

    def one_head(head_no):
        query_one = lax.dynamic_index_in_dim(queries, head_no, 1, keepdims=False)
        key_one = lax.dynamic_index_in_dim(rotated_keys, head_no // query_group_width, 1, keepdims=False)
        value_one = lax.dynamic_index_in_dim(repeated_values, head_no // query_group_width, 1, keepdims=False)
        scores = jnp.dot(query_one, key_one.T, preferred_element_type=jnp.float32) / jnp.sqrt(jnp.float32(HEAD_SIZE))
        scores = jnp.where(allowed, scores, -jnp.inf)
        row_max = lax.optimization_barrier(jnp.max(scores, axis=1, keepdims=True))
        exp_terms = jnp.exp(scores - row_max)
        prob_bf = (exp_terms / lax.optimization_barrier(jnp.sum(exp_terms, axis=1, keepdims=True))).astype(jnp.bfloat16)
        return jnp.dot(prob_bf, value_one, preferred_element_type=jnp.float32).astype(jnp.bfloat16)
    heads_out = lax.map(one_head, jnp.arange(QUERY_HEADS, dtype=jnp.int32))
    heads_out = jnp.transpose(heads_out, (1, 0, 2)).reshape(PICKED_TOKENS, QUERY_HEADS * HEAD_SIZE)
    head_width = QUERY_HEADS * HEAD_SIZE // N_CTX

    def add_attn(block_no, total):
        first_row = (block_no * head_width).astype(jnp.int32)
        left = lax.dynamic_slice_in_dim(heads_out, first_row, head_width, 1)
        right = lax.dynamic_slice_in_dim(output_weight, first_row, head_width, 0)
        return total + rounded(jnp.dot(left, right, preferred_element_type=jnp.float32))
    attn_sum = lax.fori_loop(0, N_CTX, add_attn, jnp.zeros((PICKED_TOKENS, MODEL_WIDTH), jnp.float32))
    mixed = picked_rows.astype(jnp.float32) + attn_sum
    normed_ffn = rms_scale(mixed, ffn_gain).astype(jnp.bfloat16)
    unit_width = FF // N_CTX

    def add_ffn(block_no, total):
        first_row = (block_no * unit_width).astype(jnp.int32)
        gate_proj = jnp.dot(normed_ffn, lax.dynamic_slice_in_dim(gate_weight, first_row, unit_width, 1), preferred_element_type=jnp.float32)
        up_proj = jnp.dot(normed_ffn, lax.dynamic_slice_in_dim(up_weight, first_row, unit_width, 1), preferred_element_type=jnp.float32)
        hidden = (jax.nn.silu(gate_proj) * up_proj).astype(jnp.bfloat16)
        return total + rounded(jnp.dot(hidden, lax.dynamic_slice_in_dim(down_weight, first_row, unit_width, 0), preferred_element_type=jnp.float32))
    ffn_sum = lax.fori_loop(0, N_CTX, add_ffn, jnp.zeros((PICKED_TOKENS, MODEL_WIDTH), jnp.float32))
    final = (picked_rows.astype(jnp.float32) + scales[:, None] * (attn_sum + ffn_sum)).astype(jnp.bfloat16)
    return tokens.at[picked_index].set(final)
```

```python
import jax
import jax.numpy as jnp
from jax import lax
from jax.sharding import PartitionSpec as P

QUERY_HEADS = 32
KEY_VALUE_HEADS = 8
HEAD_SIZE = 128
PICK_DEV = 16
MOST = 32
NEAR = 4

norm_eps = 1e-05
rope_base = 500000.0

f32 = jnp.float32
bf16 = jnp.bfloat16


def swap(value, mask):
    size = lax.axis_size("ctx")
    return lax.ppermute(value, "ctx", [(i, i ^ mask) for i in range(size)])


def at(stack, index):
    return lax.dynamic_index_in_dim(stack, index, 0, keepdims=False)


def dot(a, b):
    return jnp.dot(a, b, preferred_element_type=f32)


def rms_scale(matrix, gain_vec):
    mean_square = jnp.mean(matrix * matrix, axis=-1, keepdims=True)
    return matrix * lax.rsqrt(mean_square + norm_eps) * gain_vec


def quarters(matrix):
    rows, cols = matrix.shape
    return [matrix[:, a * (cols // NEAR) : (a + 1) * (cols // NEAR)] for a in range(NEAR)]


def near_scatter(matrix, near):
    stack = jnp.stack(quarters(matrix))
    total = at(stack, near).astype(f32)
    for k in (3, 1, 2):
        total = total + swap(at(stack, near ^ k), k).astype(f32)
    return total


def near_gather(block, near):
    stack = jnp.stack([block] + [swap(block, k) for k in (1, 2, 3)])
    return jnp.concatenate([at(stack, near ^ a) for a in range(NEAR)], axis=1)


def far_sum(block, far_size):
    sent = block.astype(bf16)
    total = sent.astype(f32)
    for k in range(1, far_size):
        total = total + swap(sent, NEAR * k).astype(f32)
    return total


def body(
    tokens,
    pick_flags,
    gate_scales,
    attn_gain,
    query_weight,
    key_weight,
    value_matrix,
    output_weight,
    ffn_gain,
    gate_weight,
    up_weight,
    down_weight,
):
    tok_local, width = tokens.shape
    size = lax.axis_size("ctx")
    far_size = size // NEAR
    me = lax.axis_index("ctx")
    near = me % NEAR
    far = me // NEAR
    picked_count = PICK_DEV * size
    quarter = width // NEAR

    token_ids = jnp.arange(tok_local, dtype=jnp.int32)
    upto = (token_ids[:, None] <= token_ids[None, :]).astype(bf16)
    slot_of = dot(pick_flags.astype(bf16)[None, :], upto).astype(jnp.int32)[0] - 1
    match = (jnp.arange(MOST, dtype=jnp.int32)[:, None] == slot_of[None, :]) & (pick_flags[None, :] == 1)
    hot = match.astype(bf16)
    local_index = jnp.sum(jnp.where(match, token_ids[None, :] + 1, 0), axis=1) - 1
    rows_here = dot(hot, tokens).astype(bf16)
    meta = jnp.broadcast_to(local_index.astype(bf16)[:, None], (MOST, 128))
    parts = jnp.stack([jnp.concatenate((part, meta), axis=1) for part in quarters(rows_here)])

    near_rows = jnp.concatenate([at(parts, near)] + [swap(at(parts, near ^ k), k) for k in (1, 2, 3)], axis=0)
    all_rows = jnp.concatenate([near_rows] + [swap(near_rows, NEAR * k) for k in range(1, far_size)], axis=0)
    slots = size * MOST
    all_index = all_rows[:, quarter].astype(jnp.int32)
    order = jnp.arange(slots, dtype=jnp.int32)
    device_of = (far ^ (order // (NEAR * MOST))) * NEAR + (near ^ (order // MOST % NEAR))
    taken = (all_index >= 0).astype(f32)
    earlier = (device_of[:, None] < device_of[None, :]).astype(f32)
    rank_of = jnp.sum(earlier * taken[:, None], axis=0).astype(jnp.int32) + order % MOST
    pick_ids = jnp.arange(picked_count, dtype=jnp.int32)
    select = (pick_ids[:, None] == rank_of[None, :]) & (all_index >= 0)[None, :]
    token_positions = jnp.sum(jnp.where(select, (device_of * tok_local + all_index)[None, :], 0), axis=1)
    select = select.astype(bf16)
    rows_quarter = dot(select, all_rows[:, :quarter]).astype(bf16)
    picked_rows = near_gather(rows_quarter, near)

    normalized_rows = rms_scale(picked_rows.astype(f32), attn_gain).astype(bf16)
    heads_here = query_weight.shape[1] // HEAD_SIZE
    group_width = QUERY_HEADS // KEY_VALUE_HEADS
    kv_here = max(1, heads_here // group_width)
    kv_weight = jnp.concatenate((key_weight, value_matrix), axis=1)
    kv_cols = jnp.einsum("pd,dc->cp", normalized_rows, kv_weight, preferred_element_type=f32).astype(bf16)
    comps = key_weight.shape[1] // KEY_VALUE_HEADS
    kv_cols = kv_cols.reshape(2, comps, KEY_VALUE_HEADS, picked_count)
    sends = []
    for target in range(size):
        first = target * heads_here // group_width
        sends.append(kv_cols[:, :, first : first + kv_here])
    sends = jnp.stack(sends).reshape(far_size, NEAR, 2 * comps * kv_here, picked_count)
    sends = jnp.transpose(sends, (1, 0, 2, 3))
    got = jnp.stack([at(sends, near)] + [swap(at(sends, near ^ k), k) for k in (1, 2, 3)])
    got = jnp.transpose(got, (1, 0, 2, 3))
    got = jnp.stack([at(got, far)] + [swap(at(got, far ^ k), NEAR * k) for k in range(1, far_size)])
    ordered = jnp.stack(
        [at(at(got, far ^ (d // NEAR)), near ^ (d % NEAR)) for d in range(size)]
    ).reshape(size, 2, comps, kv_here, picked_count)
    ordered = jnp.transpose(ordered, (1, 3, 0, 2, 4)).reshape(2, kv_here, HEAD_SIZE, picked_count)

    half_dim = HEAD_SIZE // 2
    frequency = rope_base ** (-(jnp.arange(half_dim, dtype=f32) * 2.0) / HEAD_SIZE)
    positions = token_positions.astype(f32)
    angles = positions[:, None] * frequency[None, :]
    cosine, sine = jnp.cos(angles), jnp.sin(angles)
    raw_q = dot(normalized_rows, query_weight).reshape(picked_count, heads_here, HEAD_SIZE)
    low, high = raw_q[..., :half_dim], raw_q[..., half_dim:]
    queries = jnp.concatenate(
        (
            low * cosine[:, None, :] - high * sine[:, None, :],
            high * cosine[:, None, :] + low * sine[:, None, :],
        ),
        axis=-1,
    ).astype(bf16)
    raw_k = ordered[0].astype(f32)
    low, high = raw_k[:, :half_dim], raw_k[:, half_dim:]
    keys = jnp.concatenate(
        (low * cosine.T - high * sine.T, high * cosine.T + low * sine.T), axis=1
    ).astype(bf16)
    values = ordered[1]
    shared = heads_here // kv_here
    queries = queries.reshape(picked_count, kv_here, shared, HEAD_SIZE)
    scores = jnp.einsum("qgsd,gdk->gsqk", queries, keys, preferred_element_type=f32) / jnp.sqrt(f32(HEAD_SIZE))
    allowed = pick_ids[None, :] <= pick_ids[:, None]
    scores = jnp.where(allowed, scores, -jnp.inf)
    row_max = jnp.max(scores, axis=-1, keepdims=True)
    exp_terms = jnp.exp(scores - row_max)
    probs = (exp_terms / jnp.sum(exp_terms, axis=-1, keepdims=True)).astype(bf16)
    head_out = jnp.einsum("gsqk,gdk->qgsd", probs, values, preferred_element_type=f32).astype(bf16)
    head_out = head_out.reshape(picked_count, heads_here * HEAD_SIZE)

    attn_quarter = far_sum(near_scatter(dot(head_out, output_weight).astype(bf16), near), far_size)
    mixed_quarter = rows_quarter.astype(f32) + attn_quarter
    mixed = near_gather(mixed_quarter.astype(bf16), near)
    normed_ffn = rms_scale(mixed.astype(f32), ffn_gain).astype(bf16)
    gate_proj = dot(normed_ffn, gate_weight)
    up_proj = dot(normed_ffn, up_weight)
    hidden = (jax.nn.silu(gate_proj) * up_proj).astype(bf16)
    ffn_part = near_scatter(dot(hidden, down_weight).astype(bf16), near).astype(bf16)

    spread = select.reshape(picked_count, far_size, NEAR * MOST)
    delta = dot(spread[:, 0].T, ffn_part) + dot(spread[:, 0].T, attn_quarter.astype(bf16))
    for k in range(1, far_size):
        delta = delta + swap(dot(spread[:, k].T, ffn_part).astype(bf16), NEAR * k).astype(f32)
    delta = delta.astype(bf16).reshape(NEAR, MOST, quarter)
    back = jnp.stack([delta[0]] + [swap(delta[k], k) for k in (1, 2, 3)])
    back = jnp.concatenate([at(back, near ^ a) for a in range(NEAR)], axis=1)
    spread_back = dot(hot.T, back)
    final = tokens.astype(f32) + gate_scales.astype(f32)[:, None] * spread_back
    return jnp.where(pick_flags[:, None] == 1, final.astype(bf16), tokens)


def solution(mesh):
    in_specs = (
        P(("dp", "ctx"), None),
        P(("dp", "ctx")),
        P(("dp", "ctx")),
        P(),
        P(None, "ctx"),
        P(None, "ctx"),
        P(None, "ctx"),
        P("ctx", None),
        P(),
        P(None, "ctx"),
        P(None, "ctx"),
        P("ctx", None),
    )
    out_specs = P(("dp", "ctx"), None)
    return jax.shard_map(body, mesh=mesh, in_specs=in_specs, out_specs=out_specs, check_vma=False)
```

```python
import jax
import jax.numpy as jnp
from jax import lax
from jax.sharding import PartitionSpec as P

QUERY_HEADS = 32
KEY_VALUE_HEADS = 8
HEAD_SIZE = 128
PICK_DEV = 16
MOST = 32
NEAR = 4

norm_eps = 1e-05
rope_base = 500000.0

f32 = jnp.float32
bf16 = jnp.bfloat16


def swap(value, mask):
    size = lax.axis_size("ctx")
    return lax.ppermute(value, "ctx", [(i, i ^ mask) for i in range(size)])


def far_mask(k):
    return NEAR * k ^ (k & 1) * 2


def quarter_of(device):
    return (device & 3) ^ ((device // NEAR & 1) * 2)


def at(stack, index):
    return lax.dynamic_index_in_dim(stack, index, 0, keepdims=False)


def dot(a, b):
    return jnp.dot(a, b, preferred_element_type=f32)


def rms_scale(matrix, gain_vec):
    mean_square = jnp.mean(matrix * matrix, axis=-1, keepdims=True)
    return matrix * lax.rsqrt(mean_square + norm_eps) * gain_vec


def quarters(matrix):
    rows, cols = matrix.shape
    return [matrix[:, a * (cols // NEAR) : (a + 1) * (cols // NEAR)] for a in range(NEAR)]


def near_scatter(matrix, near):
    stack = jnp.stack(quarters(matrix))
    total = at(stack, near).astype(f32)
    for k in (3, 1, 2):
        total = total + swap(at(stack, near ^ k), k).astype(f32)
    return total


def near_gather(block, near):
    stack = jnp.stack([block] + [swap(block, k) for k in (1, 2, 3)])
    return jnp.concatenate([at(stack, near ^ a) for a in range(NEAR)], axis=1)


def far_sum(block, far_size):
    sent = block.astype(bf16)
    total = sent.astype(f32)
    for k in range(1, far_size):
        total = total + swap(sent, far_mask(k)).astype(f32)
    return total


def body(
    tokens,
    pick_flags,
    gate_scales,
    attn_gain,
    query_weight,
    key_weight,
    value_matrix,
    output_weight,
    ffn_gain,
    gate_weight,
    up_weight,
    down_weight,
):
    tok_local, width = tokens.shape
    size = lax.axis_size("ctx")
    far_size = size // NEAR
    me = lax.axis_index("ctx")
    far = me // NEAR
    near = quarter_of(me)
    picked_count = PICK_DEV * size
    quarter = width // NEAR

    token_ids = jnp.arange(tok_local, dtype=jnp.int32)
    upto = (token_ids[:, None] <= token_ids[None, :]).astype(bf16)
    slot_of = dot(pick_flags.astype(bf16)[None, :], upto).astype(jnp.int32)[0] - 1
    match = (jnp.arange(MOST, dtype=jnp.int32)[:, None] == slot_of[None, :]) & (pick_flags[None, :] == 1)
    hot = match.astype(bf16)
    local_index = jnp.sum(jnp.where(match, token_ids[None, :] + 1, 0), axis=1) - 1
    rows_here = dot(hot, tokens).astype(bf16)
    meta = jnp.broadcast_to(local_index.astype(bf16)[:, None], (MOST, 128))
    parts = jnp.stack([jnp.concatenate((part, meta), axis=1) for part in quarters(rows_here)])

    near_rows = jnp.concatenate([at(parts, near)] + [swap(at(parts, near ^ k), k) for k in (1, 2, 3)], axis=0)
    all_rows = jnp.concatenate([near_rows] + [swap(near_rows, far_mask(k)) for k in range(1, far_size)], axis=0)
    slots = size * MOST
    all_index = all_rows[:, quarter].astype(jnp.int32)
    order = jnp.arange(slots, dtype=jnp.int32)
    far_of = far ^ (order // (NEAR * MOST))
    device_of = far_of * NEAR + (near ^ (order // MOST % NEAR) ^ (far_of & 1) * 2)
    taken = (all_index >= 0).astype(f32)
    earlier = (device_of[:, None] < device_of[None, :]).astype(f32)
    rank_of = jnp.sum(earlier * taken[:, None], axis=0).astype(jnp.int32) + order % MOST
    pick_ids = jnp.arange(picked_count, dtype=jnp.int32)
    select = (pick_ids[:, None] == rank_of[None, :]) & (all_index >= 0)[None, :]
    token_positions = jnp.sum(jnp.where(select, (device_of * tok_local + all_index)[None, :], 0), axis=1)
    select = select.astype(bf16)
    rows_quarter = dot(select, all_rows[:, :quarter]).astype(bf16)
    picked_rows = near_gather(rows_quarter, near)

    normalized_rows = rms_scale(picked_rows.astype(f32), attn_gain).astype(bf16)
    heads_here = query_weight.shape[1] // HEAD_SIZE
    group_width = QUERY_HEADS // KEY_VALUE_HEADS
    kv_here = max(1, heads_here // group_width)
    kv_weight = jnp.concatenate((key_weight, value_matrix), axis=1)
    kv_cols = jnp.einsum("pd,dc->cp", normalized_rows, kv_weight, preferred_element_type=f32).astype(bf16)
    comps = key_weight.shape[1] // KEY_VALUE_HEADS
    kv_cols = kv_cols.reshape(2, comps, KEY_VALUE_HEADS, picked_count)
    sends = []
    for label in range(NEAR):
        for group in range(far_size):
            target = group * NEAR + (label ^ (group & 1) * 2)
            first = target * heads_here // group_width
            sends.append(kv_cols[:, :, first : first + kv_here])
    sends = jnp.stack(sends).reshape(NEAR, far_size, 2 * comps * kv_here, picked_count)
    got = jnp.stack([at(sends, near)] + [swap(at(sends, near ^ k), k) for k in (1, 2, 3)])
    got = jnp.transpose(got, (1, 0, 2, 3))
    got = jnp.stack([at(got, far)] + [swap(at(got, far ^ k), far_mask(k)) for k in range(1, far_size)])
    ordered = jnp.stack(
        [at(at(got, far ^ (d // NEAR)), near ^ quarter_of(d)) for d in range(size)]
    ).reshape(size, 2, comps, kv_here, picked_count)
    ordered = jnp.transpose(ordered, (1, 3, 0, 2, 4)).reshape(2, kv_here, HEAD_SIZE, picked_count)

    half_dim = HEAD_SIZE // 2
    frequency = rope_base ** (-(jnp.arange(half_dim, dtype=f32) * 2.0) / HEAD_SIZE)
    positions = token_positions.astype(f32)
    angles = positions[:, None] * frequency[None, :]
    cosine, sine = jnp.cos(angles), jnp.sin(angles)
    raw_q = dot(normalized_rows, query_weight).reshape(picked_count, heads_here, HEAD_SIZE)
    low, high = raw_q[..., :half_dim], raw_q[..., half_dim:]
    queries = jnp.concatenate(
        (
            low * cosine[:, None, :] - high * sine[:, None, :],
            high * cosine[:, None, :] + low * sine[:, None, :],
        ),
        axis=-1,
    ).astype(bf16)
    raw_k = ordered[0].astype(f32)
    low, high = raw_k[:, :half_dim], raw_k[:, half_dim:]
    keys = jnp.concatenate(
        (low * cosine.T - high * sine.T, high * cosine.T + low * sine.T), axis=1
    ).astype(bf16)
    values = ordered[1]
    shared = heads_here // kv_here
    queries = queries.reshape(picked_count, kv_here, shared, HEAD_SIZE)
    scores = jnp.einsum("qgsd,gdk->gsqk", queries, keys, preferred_element_type=f32) / jnp.sqrt(f32(HEAD_SIZE))
    allowed = pick_ids[None, :] <= pick_ids[:, None]
    scores = jnp.where(allowed, scores, -jnp.inf)
    row_max = jnp.max(scores, axis=-1, keepdims=True)
    exp_terms = jnp.exp(scores - row_max)
    probs = (exp_terms / jnp.sum(exp_terms, axis=-1, keepdims=True)).astype(bf16)
    head_out = jnp.einsum("gsqk,gdk->qgsd", probs, values, preferred_element_type=f32).astype(bf16)
    head_out = head_out.reshape(picked_count, heads_here * HEAD_SIZE)

    attn_quarter = far_sum(near_scatter(dot(head_out, output_weight).astype(bf16), near), far_size)
    mixed_quarter = rows_quarter.astype(f32) + attn_quarter
    mixed = near_gather(mixed_quarter.astype(bf16), near)
    normed_ffn = rms_scale(mixed.astype(f32), ffn_gain).astype(bf16)
    gate_proj = dot(normed_ffn, gate_weight)
    up_proj = dot(normed_ffn, up_weight)
    hidden = (jax.nn.silu(gate_proj) * up_proj).astype(bf16)
    ffn_part = near_scatter(dot(hidden, down_weight).astype(bf16), near).astype(bf16)

    spread = select.reshape(picked_count, far_size, NEAR * MOST)
    delta = dot(spread[:, 0].T, ffn_part) + dot(spread[:, 0].T, attn_quarter.astype(bf16))
    for k in range(1, far_size):
        delta = delta + swap(dot(spread[:, k].T, ffn_part).astype(bf16), far_mask(k)).astype(f32)
    delta = delta.astype(bf16).reshape(NEAR, MOST, quarter)
    back = jnp.stack([delta[0]] + [swap(delta[k], k) for k in (1, 2, 3)])
    back = jnp.concatenate([at(back, near ^ a) for a in range(NEAR)], axis=1)
    spread_back = dot(hot.T, back)
    final = tokens.astype(f32) + gate_scales.astype(f32)[:, None] * spread_back
    return jnp.where(pick_flags[:, None] == 1, final.astype(bf16), tokens)


def solution(mesh):
    in_specs = (
        P(("dp", "ctx"), None),
        P(("dp", "ctx")),
        P(("dp", "ctx")),
        P(),
        P(None, "ctx"),
        P(None, "ctx"),
        P(None, "ctx"),
        P("ctx", None),
        P(),
        P(None, "ctx"),
        P(None, "ctx"),
        P("ctx", None),
    )
    out_specs = P(("dp", "ctx"), None)
    return jax.shard_map(body, mesh=mesh, in_specs=in_specs, out_specs=out_specs, check_vma=False)
```

```python
import functools

import jax
import jax.numpy as jnp
from jax import lax
from jax.experimental import pallas as pl
from jax.experimental.pallas import tpu as pltpu
from jax.sharding import PartitionSpec as P

QUERY_HEADS = 32
KEY_VALUE_HEADS = 8
HEAD_SIZE = 128
PICK_DEV = 16
MOST = 32
NEAR = 4
META = 128

norm_eps = 1e-05
rope_base = 500000.0

f32 = jnp.float32
bf16 = jnp.bfloat16
i32 = jnp.int32

VMEM = pl.BlockSpec(memory_space=pltpu.VMEM)
SMEM = pl.BlockSpec(memory_space=pltpu.SMEM)
ANY = pl.BlockSpec(memory_space=pl.ANY)
HBM = pl.BlockSpec(memory_space=pltpu.HBM)
MIB = 1024 * 1024


def swap(value, mask):
    size = lax.axis_size("ctx")
    return lax.ppermute(value, "ctx", [(i, i ^ mask) for i in range(size)])


def far_mask(k):
    return NEAR * k ^ (k & 1) * 2


def quarter_of(device):
    return (device & 3) ^ ((device // NEAR & 1) * 2)


def dot(a, b):
    return jnp.dot(a, b, preferred_element_type=f32)


def dot_nt(a, b):
    return lax.dot_general(a, b, (((1,), (1,)), ((), ())), preferred_element_type=f32)


def dot_tn(a, b):
    return lax.dot_general(a, b, (((0,), (0,)), ((), ())), preferred_element_type=f32)


def span(index, width):
    return pl.ds(pl.multiple_of(index * width, width), width)


def shape(dims, dtype=bf16):
    return jax.ShapeDtypeStruct(dims, dtype)


def run(kernel, name, out_shape, specs, *args, scratch=(), limit=8):
    outs = jax.tree.map(lambda _: VMEM, out_shape)
    return pl.pallas_call(
        kernel,
        in_specs=specs,
        out_specs=outs,
        out_shape=out_shape,
        scratch_shapes=scratch,
        compiler_params=pltpu.CompilerParams(vmem_limit_bytes=limit * MIB),
        name=name,
    )(*args)


def load(weights, after, name):
    count = len(weights)

    def kernel(*refs):
        sources, targets, done, sems = refs[:count], refs[count + 1 : -2], refs[-2], refs[-1]
        copies = [
            pltpu.make_async_copy(source, target, sems.at[i])
            for i, (source, target) in enumerate(zip(sources, targets))
        ]
        for copy in copies:
            copy.start()
        for copy in copies:
            copy.wait()
        done[...] = jnp.zeros_like(done)

    return pl.pallas_call(
        kernel,
        in_specs=[HBM] * count + [ANY],
        out_specs=[VMEM] * (count + 1),
        out_shape=[pltpu.VMEM(w.shape, w.dtype) for w in weights] + [pltpu.VMEM((8, 128), i32)],
        scratch_shapes=[pltpu.SemaphoreType.DMA((count,))],
        compiler_params=pltpu.CompilerParams(vmem_limit_bytes=MIB),
        name=name,
    )(*[pltpu.with_memory_space_constraint(w, pltpu.HBM) for w in weights], after)


def slots_of(flags):
    tokens = flags.shape[1]
    flag = jnp.broadcast_to(flags.astype(f32), (MOST, tokens))
    upto = lax.broadcasted_iota(i32, (tokens, tokens), 0) <= lax.broadcasted_iota(i32, (tokens, tokens), 1)
    place = dot(flag.astype(bf16), upto.astype(f32).astype(bf16))
    slot = lax.broadcasted_iota(i32, (MOST, tokens), 0).astype(f32) + 1.0
    return jnp.where((place == slot) & (flag > 0.5), 1.0, 0.0)


def pick_kernel(near, flags, tokens, *outs):
    hot = slots_of(flags[...])
    number = lax.broadcasted_iota(i32, hot.shape, 1).astype(f32) + 1.0
    index = jnp.sum(hot * number, axis=1, keepdims=True) - 1.0
    meta = jnp.broadcast_to(index, (MOST, META)).astype(bf16)
    hot = hot.astype(bf16)
    for k in range(NEAR):
        width = outs[k].shape[1] - META
        outs[k][:, :width] = dot(hot, tokens[:, span(near[0] ^ k, width)]).astype(bf16)
        outs[k][:, width:] = meta


def put_kernel(near, flags, scales, tokens, *refs):
    blocks, out = refs[:NEAR], refs[NEAR]
    hot = (slots_of(flags[...]) * scales[...].astype(f32)).astype(bf16)
    for k in range(NEAR):
        cols = span(near[0] ^ k, blocks[k].shape[1])
        out[:, cols] = (tokens[:, cols].astype(f32) + dot_tn(hot, blocks[k][...])).astype(bf16)


def normed(near, blocks, gain, out):
    width = out.shape[1]
    total = 0.0
    for block in blocks:
        value = block[...].astype(f32)
        total += jnp.sum(value * value, axis=1, keepdims=True)
    scale = lax.rsqrt(total * (1.0 / width) + norm_eps)
    for k, block in enumerate(blocks):
        cols = span(near[0] ^ k, block.shape[1])
        out[:, cols] = (block[...].astype(f32) * scale * gain[:, cols]).astype(bf16)


def kv_kernel(near, b0, b1, b2, b3, gain, key_weight, value_weight, place_k, place_v, done, rows, s0, s1, s2, s3):
    normed(near, (b0, b1, b2, b3), gain, rows)
    keys = dot(rows[...], key_weight[...]).astype(bf16)
    values = dot(rows[...], value_weight[...]).astype(bf16)
    sends = (dot_nt(place_k[...], keys) + dot_nt(place_v[...], values)).astype(bf16)
    height = s0.shape[0]
    for k, out in enumerate((s0, s1, s2, s3)):
        out[...] = sends[k * height : (k + 1) * height]


def matmul_kernel(left, right, out):
    out[...] = dot(left[...], right[...]).astype(out.dtype)


def attention_kernel(raw_q, raw_kv, order_k, order_v, cos_row, sin_row, cos_col, sin_col, out):
    half = HEAD_SIZE // 2
    keys = dot(order_k[...], raw_kv[...])
    values = dot(order_v[...], raw_kv[...]).astype(bf16)
    low, high = keys[:half], keys[half:]
    cosine, sine = cos_col[...], sin_col[...]
    keys = jnp.concatenate((low * cosine - high * sine, high * cosine + low * sine), axis=0).astype(bf16)
    count = raw_q.shape[0]
    allowed = lax.broadcasted_iota(i32, (count, count), 1) <= lax.broadcasted_iota(i32, (count, count), 0)
    for head in range(raw_q.shape[1] // HEAD_SIZE):
        cols = slice(head * HEAD_SIZE, (head + 1) * HEAD_SIZE)
        query = raw_q[:, cols]
        query = (query * cos_row[...] + pltpu.roll(query, half, 1) * sin_row[...]).astype(bf16)
        scores = dot(query, keys) * (1.0 / HEAD_SIZE**0.5)
        scores = jnp.where(allowed, scores, -jnp.inf)
        terms = jnp.exp(scores - jnp.max(scores, axis=1, keepdims=True))
        probs = (terms / jnp.sum(terms, axis=1, keepdims=True)).astype(bf16)
        out[:, cols] = dot_nt(probs, values).astype(bf16)


def block_kernel(k, near, left, right, out):
    out[...] = dot(left[...], right[:, span(near[0] ^ k, out.shape[1])]).astype(bf16)


def hidden_kernel(near, b0, b1, b2, b3, gain, gate, up, out, rows):
    normed(near, (b0, b1, b2, b3), gain, rows)
    gate_proj = dot(rows[...], gate[...])
    up_proj = dot(rows[...], up[...])
    out[...] = (jax.nn.silu(gate_proj) * up_proj).astype(bf16)


def column_blocks(near_arr, left, right, name):
    count, quarter = left.shape[0], right.shape[1] // NEAR
    outs = {}
    for k in (3, 1, 2, 0):
        outs[k] = run(
            functools.partial(block_kernel, k), name, shape((count, quarter)), [SMEM, VMEM, VMEM], near_arr, left, right
        )
    return outs


def near_scatter(blocks):
    total = blocks[0].astype(f32)
    for k in (3, 1, 2):
        total = total + swap(blocks[k], k).astype(f32)
    return total


def far_sum(block, far_size):
    sent = block.astype(bf16)
    total = sent.astype(f32)
    for k in range(1, far_size):
        total = total + swap(sent, far_mask(k)).astype(f32)
    return total


def body(
    tokens,
    pick_flags,
    gate_scales,
    attn_gain,
    query_weight,
    key_weight,
    value_matrix,
    output_weight,
    ffn_gain,
    gate_weight,
    up_weight,
    down_weight,
):
    tok_local, width = tokens.shape
    size = lax.axis_size("ctx")
    far_size = size // NEAR
    me = lax.axis_index("ctx")
    far = me // NEAR
    near = quarter_of(me)
    near_arr = near.astype(i32).reshape(1)
    count = PICK_DEV * size
    quarter = width // NEAR
    kernel_mib = 8 if count <= 128 else 24
    flags_row = pick_flags.reshape(1, tok_local)
    attn_gain, ffn_gain = attn_gain.reshape(1, width), ffn_gain.reshape(1, width)

    parts = run(
        pick_kernel, "pick", [shape((MOST, quarter + META))] * NEAR, [SMEM, VMEM, VMEM], near_arr, flags_row, tokens
    )
    key_w, value_w, query_w, done = load((key_weight, value_matrix, query_weight), parts[0], "load_qkv")

    near_rows = jnp.concatenate([parts[0]] + [swap(parts[k], k) for k in (1, 2, 3)], axis=0)
    gate_w, done = load((gate_weight,), near_rows, "load_gate")
    all_rows = jnp.concatenate([near_rows] + [swap(near_rows, far_mask(k)) for k in range(1, far_size)], axis=0)
    slots = size * MOST
    all_index = all_rows[:, quarter].astype(i32)
    order = jnp.arange(slots, dtype=i32)
    far_of = far ^ (order // (NEAR * MOST))
    device_of = far_of * NEAR + (near ^ (order // MOST % NEAR) ^ (far_of & 1) * 2)
    taken = (all_index >= 0).astype(f32)
    earlier = (device_of[:, None] < device_of[None, :]).astype(f32)
    rank_of = jnp.sum(earlier * taken[:, None], axis=0).astype(i32) + order % MOST + done[0, 0]
    pick_ids = jnp.arange(count, dtype=i32)
    select = (pick_ids[:, None] == rank_of[None, :]) & (all_index >= 0)[None, :]
    token_positions = jnp.sum(jnp.where(select, (device_of * tok_local + all_index)[None, :], 0), axis=1)
    select = select.astype(bf16)
    rows_quarter = dot(select, all_rows[:, :quarter]).astype(bf16)
    output_w, done = load((output_weight,), rows_quarter, "load_out")
    row_blocks = [rows_quarter] + [swap(rows_quarter, k) for k in (1, 2, 3)]

    half_dim = HEAD_SIZE // 2
    frequency = rope_base ** (-(jnp.arange(half_dim, dtype=f32) * 2.0) / HEAD_SIZE)
    angles = token_positions.astype(f32)[:, None] * frequency[None, :]
    cosine, sine = jnp.cos(angles), jnp.sin(angles)
    cos_row = jnp.concatenate((cosine, cosine), axis=1)
    sin_row = jnp.concatenate((-sine, sine), axis=1)

    comps = key_weight.shape[1] // KEY_VALUE_HEADS
    heads_here = query_weight.shape[1] // HEAD_SIZE
    group_width = QUERY_HEADS // KEY_VALUE_HEADS
    block_rows = 2 * comps
    total_rows = size * block_rows
    row_id = jnp.arange(total_rows, dtype=i32)
    comp_id, is_value = row_id % comps, row_id // comps % 2
    to_far = far ^ (row_id // block_rows % far_size)
    target = to_far * NEAR + (near ^ (row_id // (block_rows * far_size)) ^ (to_far & 1) * 2)
    column = comp_id * KEY_VALUE_HEADS + target * heads_here // group_width
    col_id = jnp.arange(key_weight.shape[1], dtype=i32)
    place = column[:, None] == col_id[None, :]
    place_k = (place & (is_value == 0)[:, None]).astype(bf16)
    place_v = (place & (is_value == 1)[:, None]).astype(bf16)
    rows_normed, *sends = run(
        kv_kernel,
        "keys_values",
        [shape((count, width))] + [shape((total_rows // NEAR, count))] * NEAR,
        [SMEM] + [VMEM] * 9 + [ANY],
        near_arr,
        *row_blocks,
        attn_gain,
        key_w,
        value_w,
        place_k,
        place_v,
        done,
        limit=kernel_mib,
    )
    got = [sends[0]] + [swap(sends[k], k) for k in (1, 2, 3)]
    raw_q = run(
        matmul_kernel, "query", shape((count, heads_here * HEAD_SIZE), f32), [VMEM, VMEM], rows_normed, query_w
    )
    pieces = []
    for k in range(far_size):
        piece = jnp.concatenate([g[k * block_rows : (k + 1) * block_rows] for g in got], axis=0)
        pieces.append(swap(piece, far_mask(k)) if k else piece)
    raw_kv = jnp.concatenate(pieces, axis=0)
    from_far = far ^ (row_id // (block_rows * NEAR))
    origin = from_far * NEAR + (near ^ (row_id // block_rows % NEAR) ^ (from_far & 1) * 2)
    ordered = jnp.arange(HEAD_SIZE, dtype=i32)[:, None] == (origin * comps + comp_id)[None, :]
    order_k = (ordered & (is_value == 0)[None, :]).astype(bf16)
    order_v = (ordered & (is_value == 1)[None, :]).astype(bf16)
    heads = run(
        attention_kernel,
        "attention",
        shape((count, heads_here * HEAD_SIZE)),
        [VMEM] * 8,
        raw_q,
        raw_kv,
        order_k,
        order_v,
        cos_row,
        sin_row,
        cosine.T,
        sine.T,
        limit=kernel_mib,
    )

    out_blocks = column_blocks(near_arr, heads, output_w, "attn_out")
    attn_near = near_scatter(out_blocks).astype(bf16)
    down_w, done = load((down_weight,), attn_near, "load_down")
    attn_quarter = far_sum(attn_near, far_size) + done[0, 0].astype(f32)
    mixed_quarter = (rows_quarter.astype(f32) + attn_quarter).astype(bf16)
    up_w, done = load((up_weight,), mixed_quarter, "load_up")
    mixed_blocks = [mixed_quarter] + [swap(mixed_quarter, k) for k in (1, 2, 3)]
    hidden = run(
        hidden_kernel,
        "hidden",
        shape((count, gate_weight.shape[1])),
        [SMEM] + [VMEM] * 7,
        near_arr,
        *mixed_blocks,
        ffn_gain,
        gate_w,
        up_w,
        scratch=[pltpu.VMEM((count, width), bf16)],
        limit=kernel_mib,
    )
    ffn_part = near_scatter(column_blocks(near_arr, hidden, down_w, "ffn_out")).astype(bf16)

    spread = select.reshape(count, far_size, NEAR * MOST)
    delta = dot_tn(spread[:, 0], ffn_part) + dot_tn(spread[:, 0], attn_quarter.astype(bf16))
    for k in range(1, far_size):
        delta = delta + swap(dot_tn(spread[:, k], ffn_part).astype(bf16), far_mask(k)).astype(f32)
    delta = delta.astype(bf16).reshape(NEAR, MOST, quarter)
    back = [delta[0]] + [swap(delta[k], k) for k in (1, 2, 3)]
    return run(
        put_kernel,
        "put",
        shape((tok_local, width)),
        [SMEM] + [VMEM] * 7,
        near_arr,
        flags_row,
        gate_scales.reshape(1, tok_local),
        tokens,
        *back,
    )


def solution(mesh):
    in_specs = (
        P(("dp", "ctx"), None),
        P(("dp", "ctx")),
        P(("dp", "ctx")),
        P(),
        P(None, "ctx"),
        P(None, "ctx"),
        P(None, "ctx"),
        P("ctx", None),
        P(),
        P(None, "ctx"),
        P(None, "ctx"),
        P("ctx", None),
    )
    out_specs = P(("dp", "ctx"), None)
    return jax.shard_map(body, mesh=mesh, in_specs=in_specs, out_specs=out_specs, check_vma=False)
```

```python
import functools

import jax
import jax.numpy as jnp
from jax import lax
from jax.experimental import pallas as pl
from jax.experimental.pallas import tpu as pltpu
from jax.sharding import PartitionSpec as P

QUERY_HEADS = 32
KEY_VALUE_HEADS = 8
HEAD_SIZE = 128
PICK_DEV = 16
MOST = 32
NEAR = 4
META = 128
FRONT_CUTS = 2
ATTN_CUTS = 2
BACK_CUTS = 2

norm_eps = 1e-05
rope_base = 500000.0

f32 = jnp.float32
bf16 = jnp.bfloat16
i32 = jnp.int32

VMEM = pl.BlockSpec(memory_space=pltpu.VMEM)
SMEM = pl.BlockSpec(memory_space=pltpu.SMEM)
ANY = pl.BlockSpec(memory_space=pl.ANY)
HBM = pl.BlockSpec(memory_space=pltpu.HBM)
MIB = 1024 * 1024


def swap(value, mask):
    size = lax.axis_size("ctx")
    return lax.ppermute(value, "ctx", [(i, i ^ mask) for i in range(size)])


def far_mask(k):
    return NEAR * k ^ (k & 1) * 2


def quarter_of(device):
    return (device & 3) ^ ((device // NEAR & 1) * 2)


def dot(a, b):
    return jnp.dot(a, b, preferred_element_type=f32)


def dot_nt(a, b):
    return lax.dot_general(a, b, (((1,), (1,)), ((), ())), preferred_element_type=f32)


def dot_tn(a, b):
    return lax.dot_general(a, b, (((0,), (0,)), ((), ())), preferred_element_type=f32)


def span(index, width):
    return pl.ds(pl.multiple_of(index * width, width), width)


def shape(dims, dtype=bf16):
    return jax.ShapeDtypeStruct(dims, dtype)


def run(kernel, name, out_shape, specs, *args, scratch=(), limit=4):
    outs = jax.tree.map(lambda _: VMEM, out_shape)
    return pl.pallas_call(
        kernel,
        in_specs=specs,
        out_specs=outs,
        out_shape=out_shape,
        scratch_shapes=scratch,
        compiler_params=pltpu.CompilerParams(vmem_limit_bytes=limit * MIB),
        name=name,
    )(*args)


def load(weights, after, name, rows=None, zeros=(8, 128)):
    count = len(weights)

    def kernel(*refs):
        sources, targets, done, sems = refs[:count], refs[count + 1 : -2], refs[-2], refs[-1]
        if rows:
            sources = [source.at[pl.ds(*rows)] for source in sources]
        copies = [
            pltpu.make_async_copy(source, target, sems.at[i])
            for i, (source, target) in enumerate(zip(sources, targets))
        ]
        for copy in copies:
            copy.start()
        for copy in copies:
            copy.wait()
        done[...] = jnp.zeros_like(done)

    return pl.pallas_call(
        kernel,
        in_specs=[HBM] * count + [ANY],
        out_specs=[VMEM] * (count + 1),
        out_shape=[pltpu.VMEM((rows[1] if rows else w.shape[0], w.shape[1]), w.dtype) for w in weights] + [pltpu.VMEM(zeros, i32)],
        scratch_shapes=[pltpu.SemaphoreType.DMA((count,))],
        compiler_params=pltpu.CompilerParams(vmem_limit_bytes=MIB),
        name=name,
    )(*[pltpu.with_memory_space_constraint(w, pltpu.HBM) for w in weights], after)


def in_vmem(value):
    return pltpu.with_memory_space_constraint(value, pltpu.VMEM)


def slots_of(flags):
    tokens = flags.shape[1]
    flag = jnp.broadcast_to(flags.astype(f32), (MOST, tokens))
    upto = lax.broadcasted_iota(i32, (tokens, tokens), 0) <= lax.broadcasted_iota(i32, (tokens, tokens), 1)
    place = dot(flag.astype(bf16), upto.astype(f32).astype(bf16))
    slot = lax.broadcasted_iota(i32, (MOST, tokens), 0).astype(f32) + 1.0
    return jnp.where((place == slot) & (flag > 0.5), 1.0, 0.0)


def pick_kernel(near, flags_hbm, tokens_hbm, *refs):
    outs, (flags, tokens, sems) = refs[:NEAR], refs[NEAR:]
    copies = [
        pltpu.make_async_copy(flags_hbm, flags, sems.at[0]),
        pltpu.make_async_copy(tokens_hbm, tokens, sems.at[1]),
    ]
    for copy in copies:
        copy.start()
    copies[0].wait()
    hot = slots_of(flags[...])
    number = lax.broadcasted_iota(i32, hot.shape, 1).astype(f32) + 1.0
    index = jnp.sum(hot * number, axis=1, keepdims=True) - 1.0
    meta = jnp.broadcast_to(index, (MOST, META)).astype(bf16)
    hot = hot.astype(bf16)
    copies[1].wait()
    for k in range(NEAR):
        width = outs[k].shape[1] - META
        outs[k][:, META:] = dot(hot, tokens[:, span(near[0] ^ k, width)]).astype(bf16)
        outs[k][:, :META] = meta


def pack_kernel(done, *refs):
    blocks, outs = refs[:NEAR], refs[NEAR:]
    start = 0
    for out in outs:
        for k, block in enumerate(blocks):
            out[k * MOST : (k + 1) * MOST] = block[:, start : start + out.shape[1]]
        start += out.shape[1]


def put_kernel(near, flags, scales, tokens, *refs):
    blocks, (out, held, sems) = refs[:NEAR], refs[NEAR:]
    hot = (slots_of(flags[...]) * scales[...].astype(f32)).astype(bf16)
    copies = []
    for k, block in enumerate(blocks):
        cols = span(near[0] ^ k, block.shape[1])
        held[:, cols] = (tokens[:, cols].astype(f32) + dot_tn(hot, block[...])).astype(bf16)
        copies.append(pltpu.make_async_copy(held.at[:, cols], out.at[:, cols], sems.at[k]))
        copies[-1].start()
    for copy in copies:
        copy.wait()


def part_cols(near, index, cuts, width):
    return span((near[0] ^ index // cuts) * cuts + index % cuts, width)


def normed(near, blocks, gain, out):
    width = out.shape[1]
    total = 0.0
    for block in blocks:
        value = block[...].astype(f32)
        total += jnp.sum(value * value, axis=1, keepdims=True)
    scale = lax.rsqrt(total * (1.0 / width) + norm_eps)
    for i, block in enumerate(blocks):
        cols = part_cols(near, i, len(blocks) // NEAR, block.shape[1])
        out[:, cols] = (block[...].astype(f32) * scale * gain[:, cols]).astype(bf16)


def kv_kernel(near, gain, key_weight, value_weight, place_k, place_v, done, *refs):
    blocks, (rows, *outs) = refs[: -1 - NEAR], refs[-1 - NEAR :]
    normed(near, blocks, gain, rows)
    keys = dot(rows[...], key_weight[...]).astype(bf16)
    values = dot(rows[...], value_weight[...]).astype(bf16)
    sends = (dot_nt(place_k[...], keys) + dot_nt(place_v[...], values)).astype(bf16)
    height = outs[0].shape[0]
    for k, out in enumerate(outs):
        out[...] = sends[k * height : (k + 1) * height]


def matmul_kernel(left, right, out):
    out[...] = dot(left[...], right[...]).astype(out.dtype)


def attention_kernel(raw_q, raw_kv, order_k, order_v, cos_row, sin_row, cos_col, sin_col, done_a, done_b, out):
    half = HEAD_SIZE // 2
    keys = dot(order_k[...], raw_kv[...])
    values = dot(order_v[...], raw_kv[...]).astype(bf16)
    low, high = keys[:half], keys[half:]
    cosine, sine = cos_col[...], sin_col[...]
    keys = jnp.concatenate((low * cosine - high * sine, high * cosine + low * sine), axis=0).astype(bf16)
    count = raw_q.shape[0]
    allowed = lax.broadcasted_iota(i32, (count, count), 1) <= lax.broadcasted_iota(i32, (count, count), 0)
    for head in range(raw_q.shape[1] // HEAD_SIZE):
        cols = slice(head * HEAD_SIZE, (head + 1) * HEAD_SIZE)
        query = raw_q[:, cols]
        query = (query * cos_row[...] + pltpu.roll(query, half, 1) * sin_row[...]).astype(bf16)
        scores = dot(query, keys) * (1.0 / HEAD_SIZE**0.5)
        scores = jnp.where(allowed, scores, -jnp.inf)
        terms = jnp.exp(scores - jnp.max(scores, axis=1, keepdims=True))
        probs = (terms / jnp.sum(terms, axis=1, keepdims=True)).astype(bf16)
        out[:, cols] = dot_nt(probs, values).astype(bf16)


def block_kernel(cuts, cut, near, left, *refs):
    rights, outs = refs[:-NEAR], refs[-NEAR:]
    depth = rights[0].shape[0]
    for k in (3, 1, 2, 0):
        cols = part_cols(near, k * cuts + cut, cuts, outs[k].shape[1])
        total = 0.0
        for i, right in enumerate(rights):
            total += dot(left[:, i * depth : (i + 1) * depth], right[:, cols])
        outs[k][...] = total.astype(bf16)


def gained(near, blocks, gain, out, cuts, cut):
    total = 0.0
    for k, block in enumerate(blocks):
        width = block.shape[1]
        value = block[...].astype(f32)
        total += jnp.sum(value * value, axis=1, keepdims=True)
        out[:, k * width : (k + 1) * width] = (value * gain[:, part_cols(near, k * cuts + cut, cuts, width)]).astype(bf16)
    return total


def cut_dot(near, rows, weight, cuts, cut):
    width = rows.shape[1] // NEAR
    total = 0.0
    for k in range(NEAR):
        depth = part_cols(near, k * cuts + cut, cuts, width)
        total += dot(rows[:, k * width : (k + 1) * width], weight[depth, :])
    return total


def hidden_part_kernel(cuts, cut, near, gain, gate, up, *refs):
    blocks, (gate_sum, up_sum, square_sum, rows) = refs[:NEAR], refs[NEAR:]
    total = gained(near, blocks, gain, rows, cuts, cut)
    square_sum[...] = jnp.broadcast_to(total, square_sum.shape)
    gate_sum[...] = cut_dot(near, rows, gate, cuts, cut)
    up_sum[...] = cut_dot(near, rows, up, cuts, cut)


def hidden_kernel(cuts, near, gain, gate, up, *refs):
    blocks, sums, (out, rows) = refs[:NEAR], refs[NEAR:-2], refs[-2:]
    total = gained(near, blocks, gain, rows, cuts, cuts - 1)
    gate_sum = cut_dot(near, rows, gate, cuts, cuts - 1)
    up_sum = cut_dot(near, rows, up, cuts, cuts - 1)
    for gate_part, up_part, square_part in zip(sums[::3], sums[1::3], sums[2::3]):
        gate_sum += gate_part[...]
        up_sum += up_part[...]
        total += square_part[:, :1]
    scale = lax.rsqrt(total * (1.0 / gate.shape[0]) + norm_eps)
    out[...] = (jax.nn.silu(gate_sum * scale) * (up_sum * scale)).astype(bf16)


def column_blocks(near_arr, left, rights, cuts, cut, name):
    dims = (left.shape[0], rights[0].shape[1] // NEAR // cuts)
    kernel = functools.partial(block_kernel, cuts, cut)
    return run(kernel, name, [shape(dims)] * NEAR, [SMEM, VMEM] + [VMEM] * len(rights), near_arr, left, *rights)


def near_gather(parts):
    got = [[part] + [swap(part, k) for k in (1, 2, 3)] for part in parts]
    return [cut[k] for k in range(NEAR) for cut in got]


def cut_cols(matrix, cuts):
    width = matrix.shape[1] // cuts
    return [matrix[:, i * width : (i + 1) * width] for i in range(cuts)]


def near_scatter(blocks):
    total = blocks[0].astype(f32)
    for k in (3, 1, 2):
        total = total + swap(blocks[k], k).astype(f32)
    return total


def far_sum(block, far_size):
    sent = block.astype(bf16)
    total = sent.astype(f32)
    for k in range(1, far_size):
        total = total + swap(sent, far_mask(k)).astype(f32)
    return total


def body(
    tokens,
    pick_flags,
    gate_scales,
    attn_gain,
    query_weight,
    key_weight,
    value_matrix,
    output_weight,
    ffn_gain,
    gate_weight,
    up_weight,
    down_weight,
):
    tok_local, width = tokens.shape
    size = lax.axis_size("ctx")
    far_size = size // NEAR
    me = lax.axis_index("ctx")
    far = me // NEAR
    near = quarter_of(me)
    near_arr = near.astype(i32).reshape(1)
    count = PICK_DEV * size
    quarter = width // NEAR
    kernel_mib = 6 if count <= 128 else 24
    flags_row = pick_flags.reshape(1, tok_local)
    attn_gain, ffn_gain = attn_gain.reshape(1, width), ffn_gain.reshape(1, width)

    parts = run(
        pick_kernel,
        "pick",
        [shape((MOST, quarter + META))] * NEAR,
        [SMEM, HBM, HBM],
        near_arr,
        pltpu.with_memory_space_constraint(flags_row, pltpu.HBM),
        pltpu.with_memory_space_constraint(tokens, pltpu.HBM),
        scratch=[
            pltpu.VMEM((1, tok_local), i32),
            pltpu.VMEM((tok_local, width), bf16),
            pltpu.SemaphoreType.DMA((2,)),
        ],
    )
    key_w, value_w, query_w, done = load((key_weight, value_matrix, query_weight), parts[0], "load_qkv")

    cuts = FRONT_CUTS
    wide = quarter // cuts
    pieces = run(
        pack_kernel,
        "pack",
        [shape((NEAR * MOST, wide + (0 if cut else META))) for cut in range(cuts)],
        [ANY] + [VMEM] * NEAR,
        done,
        *([parts[0]] + [swap(parts[k], k) for k in (1, 2, 3)]),
    )
    gate_w, done = load((gate_weight,), pieces[0], "load_gate", zeros=(1, size * MOST))
    all_rows = [
        jnp.concatenate([piece] + [swap(piece, far_mask(k)) for k in range(1, far_size)], axis=0) for piece in pieces
    ]
    slots = size * MOST
    all_index = all_rows[0][:, 0].astype(i32)
    order = jnp.arange(slots, dtype=i32)
    far_of = far ^ (order // (NEAR * MOST))
    device_of = far_of * NEAR + (near ^ (order // MOST % NEAR) ^ (far_of & 1) * 2)
    taken = (all_index >= 0).astype(f32)
    earlier = (device_of[:, None] < device_of[None, :]).astype(f32)
    rank_of = jnp.sum(earlier * taken[:, None], axis=0).astype(i32) + order % MOST + done[0]
    pick_ids = jnp.arange(count, dtype=i32)
    select = (pick_ids[:, None] == rank_of[None, :]) & (all_index >= 0)[None, :]
    token_positions = jnp.sum(jnp.where(select, (device_of * tok_local + all_index)[None, :], 0), axis=1)
    select = select.astype(bf16)
    all_rows[0] = all_rows[0][:, META:]
    row_parts = [dot(select, piece).astype(bf16) for piece in all_rows]
    output_w, up_w, done = load((output_weight, up_weight), row_parts[0], "load_out_up")
    row_blocks = near_gather(row_parts)
    rows_quarter = jnp.concatenate(row_parts, axis=1)

    half_dim = HEAD_SIZE // 2
    frequency = rope_base ** (-(jnp.arange(half_dim, dtype=f32) * 2.0) / HEAD_SIZE)
    angles = token_positions.astype(f32)[:, None] * frequency[None, :]
    cosine, sine = jnp.cos(angles), jnp.sin(angles)
    cos_row = jnp.concatenate((cosine, cosine), axis=1)
    sin_row = jnp.concatenate((-sine, sine), axis=1)

    comps = key_weight.shape[1] // KEY_VALUE_HEADS
    heads_here = query_weight.shape[1] // HEAD_SIZE
    group_width = QUERY_HEADS // KEY_VALUE_HEADS
    block_rows = 2 * comps
    total_rows = size * block_rows
    row_id = jnp.arange(total_rows, dtype=i32)
    comp_id, is_value = row_id % comps, row_id // comps % 2
    to_far = far ^ (row_id // block_rows % far_size)
    target = to_far * NEAR + (near ^ (row_id // (block_rows * far_size)) ^ (to_far & 1) * 2)
    column = comp_id * KEY_VALUE_HEADS + target * heads_here // group_width
    col_id = jnp.arange(key_weight.shape[1], dtype=i32)
    place = column[:, None] == col_id[None, :]
    place_k = (place & (is_value == 0)[:, None]).astype(bf16)
    place_v = (place & (is_value == 1)[:, None]).astype(bf16)
    rows_normed, *sends = run(
        kv_kernel,
        "keys_values",
        [shape((count, width))] + [shape((total_rows // NEAR, count))] * NEAR,
        [SMEM] + [VMEM] * 5 + [ANY] + [VMEM] * len(row_blocks),
        near_arr,
        attn_gain,
        key_w,
        value_w,
        place_k,
        place_v,
        done,
        *row_blocks,
        limit=kernel_mib,
    )
    down_half = down_weight.shape[0] // 2
    down_a, done_a = load((down_weight,), sends[0], "load_down", (0, down_half))
    got = [sends[0]] + [swap(sends[k], k) for k in (1, 2, 3)]
    raw_q = run(
        matmul_kernel, "query", shape((count, heads_here * HEAD_SIZE), f32), [VMEM, VMEM], rows_normed, query_w
    )
    pieces = []
    for k in range(far_size):
        piece = jnp.concatenate([g[k * block_rows : (k + 1) * block_rows] for g in got], axis=0)
        pieces.append(swap(piece, far_mask(k)) if k else piece)
    down_b, done_b = load((down_weight,), pieces[0], "load_down", (down_half, down_half))
    raw_kv = jnp.concatenate(pieces, axis=0)
    from_far = far ^ (row_id // (block_rows * NEAR))
    origin = from_far * NEAR + (near ^ (row_id // block_rows % NEAR) ^ (from_far & 1) * 2)
    ordered = jnp.arange(HEAD_SIZE, dtype=i32)[:, None] == (origin * comps + comp_id)[None, :]
    order_k = (ordered & (is_value == 0)[None, :]).astype(bf16)
    order_v = (ordered & (is_value == 1)[None, :]).astype(bf16)
    heads = run(
        attention_kernel,
        "attention",
        shape((count, heads_here * HEAD_SIZE)),
        [VMEM] * 8 + [ANY] * 2,
        raw_q,
        raw_kv,
        order_k,
        order_v,
        cos_row,
        sin_row,
        cosine.T,
        sine.T,
        done_a,
        done_b,
        limit=kernel_mib,
    )

    cuts = ATTN_CUTS
    attn_near = [
        near_scatter(column_blocks(near_arr, heads, (output_w,), cuts, cut, "attn_out")).astype(bf16) for cut in range(cuts)
    ]
    attn_parts = [far_sum(part, far_size) for part in attn_near]
    mixed_parts = [
        (rows.astype(f32) + part).astype(bf16) for rows, part in zip(cut_cols(rows_quarter, cuts), attn_parts)
    ]
    attn_quarter = jnp.concatenate(attn_parts, axis=1).astype(bf16)
    units = gate_weight.shape[1]
    sums = []
    for cut, part in enumerate(mixed_parts):
        blocks = near_gather([part])
        last = cut == cuts - 1
        common = dict(scratch=[pltpu.VMEM((count, width // cuts), bf16)], limit=kernel_mib)
        operands = (near_arr, ffn_gain, in_vmem(gate_w), in_vmem(up_w), *blocks)
        specs = [SMEM] + [VMEM] * (3 + NEAR)
        if not last:
            outs = [shape((count, units), f32)] * 2 + [shape((count, 128), f32)]
            kernel = functools.partial(hidden_part_kernel, cuts, cut)
            sums += run(kernel, "hidden_part", outs, specs, *operands, **common)
    kernel = functools.partial(hidden_kernel, cuts)
    hidden = run(kernel, "hidden", shape((count, units)), specs + [VMEM] * len(sums), *operands, *sums, **common)

    cuts = BACK_CUTS
    spread = select.reshape(count, far_size, NEAR * MOST)
    deltas = []
    for cut, attn_part in enumerate(cut_cols(attn_quarter, cuts)):
        blocks = column_blocks(near_arr, hidden, (in_vmem(down_a), in_vmem(down_b)), cuts, cut, "ffn_out")
        ffn_part = near_scatter(blocks).astype(bf16)
        delta = dot_tn(spread[:, 0], ffn_part) + dot_tn(spread[:, 0], attn_part)
        for k in range(1, far_size):
            delta = delta + swap(dot_tn(spread[:, k], ffn_part).astype(bf16), far_mask(k)).astype(f32)
        deltas.append(delta.astype(bf16))
    delta = jnp.concatenate(deltas, axis=1).reshape(NEAR, MOST, quarter)
    back = [delta[0]] + [swap(delta[k], k) for k in (1, 2, 3)]
    return pl.pallas_call(
        put_kernel,
        in_specs=[SMEM] + [VMEM] * (3 + NEAR),
        out_specs=HBM,
        out_shape=shape((tok_local, width)),
        scratch_shapes=[pltpu.VMEM((tok_local, width), bf16), pltpu.SemaphoreType.DMA((NEAR,))],
        compiler_params=pltpu.CompilerParams(vmem_limit_bytes=4 * MIB),
        name="put",
    )(near_arr, flags_row, gate_scales.reshape(1, tok_local), tokens, *back)


def solution(mesh):
    in_specs = (
        P(("dp", "ctx"), None),
        P(("dp", "ctx")),
        P(("dp", "ctx")),
        P(),
        P(None, "ctx"),
        P(None, "ctx"),
        P(None, "ctx"),
        P("ctx", None),
        P(),
        P(None, "ctx"),
        P(None, "ctx"),
        P("ctx", None),
    )
    out_specs = P(("dp", "ctx"), None)
    return jax.shard_map(body, mesh=mesh, in_specs=in_specs, out_specs=out_specs, check_vma=False)
```

```python
import functools

import jax
import jax.numpy as jnp
from jax import lax
from jax.experimental import pallas as pl
from jax.experimental.pallas import tpu as pltpu
from jax.sharding import PartitionSpec as P

QUERY_HEADS = 32
KEY_VALUE_HEADS = 8
HEAD_SIZE = 128
PICK_DEV = 16
MOST = 32
NEAR = 4
META = 128
INDEX_ROWS = 16
FRONT_CUTS = 2
ATTN_CUTS = 2
BACK_CUTS = 2

norm_eps = 1e-05
rope_base = 500000.0

f32 = jnp.float32
bf16 = jnp.bfloat16
i32 = jnp.int32

VMEM = pl.BlockSpec(memory_space=pltpu.VMEM)
SMEM = pl.BlockSpec(memory_space=pltpu.SMEM)
ANY = pl.BlockSpec(memory_space=pl.ANY)
HBM = pl.BlockSpec(memory_space=pltpu.HBM)
MIB = 1024 * 1024


def swap(value, mask):
    size = lax.axis_size("ctx")
    return lax.ppermute(value, "ctx", [(i, i ^ mask) for i in range(size)])


def far_mask(k):
    return NEAR * k ^ (k & 1) * 2


def quarter_of(device):
    return (device & 3) ^ ((device // NEAR & 1) * 2)


def dot(a, b):
    return jnp.dot(a, b, preferred_element_type=f32)


def dot_nt(a, b):
    return lax.dot_general(a, b, (((1,), (1,)), ((), ())), preferred_element_type=f32)


def dot_tn(a, b):
    return lax.dot_general(a, b, (((0,), (0,)), ((), ())), preferred_element_type=f32)


def span(index, width):
    return pl.ds(pl.multiple_of(index * width, width), width)


def shape(dims, dtype=bf16):
    return jax.ShapeDtypeStruct(dims, dtype)


def run(kernel, name, out_shape, specs, *args, scratch=(), limit=4):
    outs = jax.tree.map(lambda _: VMEM, out_shape)
    return pl.pallas_call(
        kernel,
        in_specs=specs,
        out_specs=outs,
        out_shape=out_shape,
        scratch_shapes=scratch,
        compiler_params=pltpu.CompilerParams(vmem_limit_bytes=limit * MIB),
        name=name,
    )(*args)


def load(weights, after, name, rows=None, zeros=(8, 128)):
    count = len(weights)

    def kernel(*refs):
        sources, targets, done, sems = refs[:count], refs[count + 1 : -2], refs[-2], refs[-1]
        if rows:
            sources = [source.at[pl.ds(*rows)] for source in sources]
        copies = [
            pltpu.make_async_copy(source, target, sems.at[i])
            for i, (source, target) in enumerate(zip(sources, targets))
        ]
        for copy in copies:
            copy.start()
        for copy in copies:
            copy.wait()
        done[...] = jnp.zeros_like(done)

    return pl.pallas_call(
        kernel,
        in_specs=[HBM] * count + [ANY],
        out_specs=[VMEM] * (count + 1),
        out_shape=[pltpu.VMEM((rows[1] if rows else w.shape[0], w.shape[1]), w.dtype) for w in weights] + [pltpu.VMEM(zeros, i32)],
        scratch_shapes=[pltpu.SemaphoreType.DMA((count,))],
        compiler_params=pltpu.CompilerParams(vmem_limit_bytes=MIB),
        name=name,
    )(*[pltpu.with_memory_space_constraint(w, pltpu.HBM) for w in weights], after)


def in_vmem(value):
    return pltpu.with_memory_space_constraint(value, pltpu.VMEM)


def slots_of(flags):
    tokens = flags.shape[1]
    flag = jnp.broadcast_to(flags.astype(f32), (MOST, tokens))
    upto = lax.broadcasted_iota(i32, (tokens, tokens), 0) <= lax.broadcasted_iota(i32, (tokens, tokens), 1)
    place = dot(flag.astype(bf16), upto.astype(f32).astype(bf16))
    slot = lax.broadcasted_iota(i32, (MOST, tokens), 0).astype(f32) + 1.0
    return jnp.where((place == slot) & (flag > 0.5), 1.0, 0.0)


def pick_kernel(near, flags_hbm, tokens_hbm, *refs):
    outs, (flags, tokens, sems) = refs[:NEAR], refs[NEAR:]
    copies = [
        pltpu.make_async_copy(flags_hbm, flags, sems.at[0]),
        pltpu.make_async_copy(tokens_hbm, tokens, sems.at[1]),
    ]
    for copy in copies:
        copy.start()
    copies[0].wait()
    hot = slots_of(flags[...])
    number = lax.broadcasted_iota(i32, hot.shape, 1).astype(f32) + 1.0
    index = jnp.sum(hot * number, axis=1, keepdims=True) - 1.0
    meta = jnp.broadcast_to(index, (MOST, META)).astype(bf16)
    hot = hot.astype(bf16)
    copies[1].wait()
    for k in range(NEAR):
        width = outs[k].shape[1] - META
        outs[k][:, META:] = dot(hot, tokens[:, span(near[0] ^ k, width)]).astype(bf16)
        outs[k][:, :META] = meta


def pack_kernel(start, wide, done, *refs):
    blocks, out = refs[:NEAR], refs[NEAR]
    for k, block in enumerate(blocks):
        out[k * MOST : (k + 1) * MOST] = block[:, start : start + wide]
    slots = NEAR * MOST
    if out.shape[0] > slots:
        index = jnp.concatenate([block[:, :slots].astype(f32) for block in blocks], axis=0)
        corner = lax.broadcasted_iota(i32, (slots, slots), 0) == lax.broadcasted_iota(i32, (slots, slots), 1)
        row = jnp.sum(jnp.where(corner, index, 0.0), axis=0, keepdims=True)
        out[slots:] = jnp.zeros((INDEX_ROWS, wide), bf16)
        out[slots:, :slots] = jnp.broadcast_to(row, (INDEX_ROWS, slots)).astype(bf16)


def put_kernel(near, flags, scales, tokens, *refs):
    blocks, (out, held, sems) = refs[:NEAR], refs[NEAR:]
    hot = (slots_of(flags[...]) * scales[...].astype(f32)).astype(bf16)
    copies = []
    for k, block in enumerate(blocks):
        cols = span(near[0] ^ k, block.shape[1])
        held[:, cols] = (tokens[:, cols].astype(f32) + dot_tn(hot, block[...])).astype(bf16)
        copies.append(pltpu.make_async_copy(held.at[:, cols], out.at[:, cols], sems.at[k]))
        copies[-1].start()
    for copy in copies:
        copy.wait()


def part_cols(near, index, cuts, width):
    return span((near[0] ^ index // cuts) * cuts + index % cuts, width)


def normed(near, blocks, gain, out):
    width = out.shape[1]
    total = 0.0
    for block in blocks:
        value = block[...].astype(f32)
        total += jnp.sum(value * value, axis=1, keepdims=True)
    scale = lax.rsqrt(total * (1.0 / width) + norm_eps)
    for i, block in enumerate(blocks):
        cols = part_cols(near, i, len(blocks) // NEAR, block.shape[1])
        out[:, cols] = (block[...].astype(f32) * scale * gain[:, cols]).astype(bf16)


def kv_kernel(near, gain, key_weight, value_weight, place_k, place_v, done, *refs):
    blocks, (rows, *outs) = refs[: -1 - NEAR], refs[-1 - NEAR :]
    normed(near, blocks, gain, rows)
    keys = dot(rows[...], key_weight[...]).astype(bf16)
    values = dot(rows[...], value_weight[...]).astype(bf16)
    sends = (dot_nt(place_k[...], keys) + dot_nt(place_v[...], values)).astype(bf16)
    height = outs[0].shape[0]
    for k, out in enumerate(outs):
        out[...] = sends[k * height : (k + 1) * height]


def matmul_kernel(left, right, out):
    out[...] = dot(left[...], right[...]).astype(out.dtype)


def attention_kernel(raw_q, raw_kv, order_k, order_v, cos_row, sin_row, cos_col, sin_col, done, out):
    half = HEAD_SIZE // 2
    keys = dot(order_k[...], raw_kv[...])
    values = dot(order_v[...], raw_kv[...]).astype(bf16)
    low, high = keys[:half], keys[half:]
    cosine, sine = cos_col[...], sin_col[...]
    keys = jnp.concatenate((low * cosine - high * sine, high * cosine + low * sine), axis=0).astype(bf16)
    count = raw_q.shape[0]
    allowed = lax.broadcasted_iota(i32, (count, count), 1) <= lax.broadcasted_iota(i32, (count, count), 0)
    for head in range(raw_q.shape[1] // HEAD_SIZE):
        cols = slice(head * HEAD_SIZE, (head + 1) * HEAD_SIZE)
        query = raw_q[:, cols]
        query = (query * cos_row[...] + pltpu.roll(query, half, 1) * sin_row[...]).astype(bf16)
        scores = dot(query, keys) * (1.0 / HEAD_SIZE**0.5)
        scores = jnp.where(allowed, scores, -jnp.inf)
        terms = jnp.exp(scores - jnp.max(scores, axis=1, keepdims=True))
        probs = (terms / jnp.sum(terms, axis=1, keepdims=True)).astype(bf16)
        out[:, cols] = dot_nt(probs, values).astype(bf16)


def block_kernel(cuts, cut, near, left, *refs):
    rights, outs = refs[:-NEAR], refs[-NEAR:]
    depth = rights[0].shape[0]
    for k in (3, 1, 2, 0):
        cols = part_cols(near, k * cuts + cut, cuts, outs[k].shape[1])
        total = 0.0
        for i, right in enumerate(rights):
            total += dot(left[:, i * depth : (i + 1) * depth], right[:, cols])
        outs[k][...] = total.astype(bf16)


def gained(near, blocks, gain, out, cuts, cut):
    total = 0.0
    for k, block in enumerate(blocks):
        width = block.shape[1]
        value = block[...].astype(f32)
        total += jnp.sum(value * value, axis=1, keepdims=True)
        out[:, k * width : (k + 1) * width] = (value * gain[:, part_cols(near, k * cuts + cut, cuts, width)]).astype(bf16)
    return total


def cut_dot(near, rows, weight, cuts, cut):
    width = rows.shape[1] // NEAR
    total = 0.0
    for k in range(NEAR):
        depth = part_cols(near, k * cuts + cut, cuts, width)
        total += dot(rows[:, k * width : (k + 1) * width], weight[depth, :])
    return total


def hidden_part_kernel(cuts, cut, near, gain, gate, up, *refs):
    blocks, (down, gate_sum, up_sum, square_sum, down_first, rows, sem) = refs[:NEAR], refs[NEAR:]
    copy = pltpu.make_async_copy(down.at[pl.ds(0, down_first.shape[0])], down_first, sem)
    copy.start()
    total = gained(near, blocks, gain, rows, cuts, cut)
    square_sum[...] = jnp.broadcast_to(total, square_sum.shape)
    gate_sum[...] = cut_dot(near, rows, gate, cuts, cut)
    up_sum[...] = cut_dot(near, rows, up, cuts, cut)
    copy.wait()


def hidden_kernel(cuts, near, gain, gate, up, *refs):
    blocks, sums, (out, rows) = refs[:NEAR], refs[NEAR:-2], refs[-2:]
    total = gained(near, blocks, gain, rows, cuts, cuts - 1)
    gate_sum = cut_dot(near, rows, gate, cuts, cuts - 1)
    up_sum = cut_dot(near, rows, up, cuts, cuts - 1)
    for gate_part, up_part, square_part in zip(sums[::3], sums[1::3], sums[2::3]):
        gate_sum += gate_part[...]
        up_sum += up_part[...]
        total += square_part[:, :1]
    scale = lax.rsqrt(total * (1.0 / gate.shape[0]) + norm_eps)
    out[...] = (jax.nn.silu(gate_sum * scale) * (up_sum * scale)).astype(bf16)


def column_blocks(near_arr, left, rights, cuts, cut, name):
    dims = (left.shape[0], rights[0].shape[1] // NEAR // cuts)
    kernel = functools.partial(block_kernel, cuts, cut)
    return run(kernel, name, [shape(dims)] * NEAR, [SMEM, VMEM] + [VMEM] * len(rights), near_arr, left, *rights)


def near_gather(parts):
    got = [[part] + [swap(part, k) for k in (1, 2, 3)] for part in parts]
    return [cut[k] for k in range(NEAR) for cut in got]


def cut_cols(matrix, cuts):
    width = matrix.shape[1] // cuts
    return [matrix[:, i * width : (i + 1) * width] for i in range(cuts)]


def near_scatter(blocks):
    total = blocks[0].astype(f32)
    for k in (3, 1, 2):
        total = total + swap(blocks[k], k).astype(f32)
    return total


def far_sum(block, far_size):
    sent = block.astype(bf16)
    total = sent.astype(f32)
    for k in range(1, far_size):
        total = total + swap(sent, far_mask(k)).astype(f32)
    return total


def body(
    tokens,
    pick_flags,
    gate_scales,
    attn_gain,
    query_weight,
    key_weight,
    value_matrix,
    output_weight,
    ffn_gain,
    gate_weight,
    up_weight,
    down_weight,
):
    tok_local, width = tokens.shape
    size = lax.axis_size("ctx")
    far_size = size // NEAR
    me = lax.axis_index("ctx")
    far = me // NEAR
    near = quarter_of(me)
    near_arr = near.astype(i32).reshape(1)
    count = PICK_DEV * size
    quarter = width // NEAR
    kernel_mib = 6 if count <= 128 else 24
    flags_row = pick_flags.reshape(1, tok_local)
    attn_gain, ffn_gain = attn_gain.reshape(1, width), ffn_gain.reshape(1, width)

    parts = run(
        pick_kernel,
        "pick",
        [shape((MOST, quarter + META))] * NEAR,
        [SMEM, HBM, HBM],
        near_arr,
        pltpu.with_memory_space_constraint(flags_row, pltpu.HBM),
        pltpu.with_memory_space_constraint(tokens, pltpu.HBM),
        scratch=[
            pltpu.VMEM((1, tok_local), i32),
            pltpu.VMEM((tok_local, width), bf16),
            pltpu.SemaphoreType.DMA((2,)),
        ],
    )
    key_w, value_w, query_w, output_w, done = load(
        (key_weight, value_matrix, query_weight, output_weight), parts[0], "load_qkvo"
    )

    cuts = FRONT_CUTS
    wide = quarter // cuts
    near_parts = [parts[0]] + [swap(parts[k], k) for k in (1, 2, 3)]
    half_slots = NEAR * MOST
    all_rows, index_rows = [], []
    for cut in range(cuts):
        piece = run(
            functools.partial(pack_kernel, META + cut * wide, wide),
            "pack",
            shape((half_slots + (0 if cut else INDEX_ROWS), wide)),
            [ANY] + [VMEM] * NEAR,
            done,
            *near_parts,
        )
        if cut == 0:
            gate_w, done = load((gate_weight,), piece, "load_gate")
        received = [piece] + [swap(piece, far_mask(k)) for k in range(1, far_size)]
        if cut == 0:
            index_rows = [rows[half_slots, :half_slots] for rows in received]
        all_rows.append(jnp.concatenate([rows[:half_slots] for rows in received], axis=0))
    slots = size * MOST
    all_index = jnp.concatenate(index_rows).astype(i32)
    order = jnp.arange(slots, dtype=i32)
    far_of = far ^ (order // (NEAR * MOST))
    device_of = far_of * NEAR + (near ^ (order // MOST % NEAR) ^ (far_of & 1) * 2)
    taken = (all_index >= 0).astype(f32)
    earlier = (device_of[:, None] < device_of[None, :]).astype(f32)
    rank_of = jnp.sum(earlier * taken[:, None], axis=0).astype(i32) + order % MOST
    pick_ids = jnp.arange(count, dtype=i32)
    select = (pick_ids[:, None] == rank_of[None, :]) & (all_index >= 0)[None, :]
    token_positions = jnp.sum(jnp.where(select, (device_of * tok_local + all_index)[None, :], 0), axis=1)
    select = select.astype(bf16)
    row_parts = [dot(select, piece).astype(bf16) for piece in all_rows]
    up_w, done = load((up_weight,), row_parts[0], "load_up")
    row_blocks = near_gather(row_parts)
    rows_quarter = jnp.concatenate(row_parts, axis=1)

    half_dim = HEAD_SIZE // 2
    frequency = rope_base ** (-(jnp.arange(half_dim, dtype=f32) * 2.0) / HEAD_SIZE)
    angles = token_positions.astype(f32)[:, None] * frequency[None, :]
    cosine, sine = jnp.cos(angles), jnp.sin(angles)
    cos_row = jnp.concatenate((cosine, cosine), axis=1)
    sin_row = jnp.concatenate((-sine, sine), axis=1)

    comps = key_weight.shape[1] // KEY_VALUE_HEADS
    heads_here = query_weight.shape[1] // HEAD_SIZE
    group_width = QUERY_HEADS // KEY_VALUE_HEADS
    block_rows = 2 * comps
    total_rows = size * block_rows
    row_id = jnp.arange(total_rows, dtype=i32)
    comp_id, is_value = row_id % comps, row_id // comps % 2
    to_far = far ^ (row_id // block_rows % far_size)
    target = to_far * NEAR + (me % NEAR ^ (row_id // (block_rows * far_size)))
    column = comp_id * KEY_VALUE_HEADS + target * heads_here // group_width
    col_id = jnp.arange(key_weight.shape[1], dtype=i32)
    place = column[:, None] == col_id[None, :]
    place_k = (place & (is_value == 0)[:, None]).astype(bf16)
    place_v = (place & (is_value == 1)[:, None]).astype(bf16)
    rows_normed, *sends = run(
        kv_kernel,
        "keys_values",
        [shape((count, width))] + [shape((total_rows // NEAR, count))] * NEAR,
        [SMEM] + [VMEM] * 5 + [ANY] + [VMEM] * len(row_blocks),
        near_arr,
        attn_gain,
        key_w,
        value_w,
        place_k,
        place_v,
        done,
        *row_blocks,
        limit=kernel_mib,
    )
    down_half = down_weight.shape[0] // 2
    got = [sends[0]] + [swap(sends[k], k) for k in (1, 2, 3)]
    raw_q = run(
        matmul_kernel, "query", shape((count, heads_here * HEAD_SIZE), f32), [VMEM, VMEM], rows_normed, query_w
    )
    pieces = []
    for k in range(far_size):
        piece = jnp.concatenate([g[k * block_rows : (k + 1) * block_rows] for g in got], axis=0)
        pieces.append(swap(piece, NEAR * k) if k else piece)
    down_b, done = load((down_weight,), pieces[0], "load_down", (down_half, down_half))
    raw_kv = jnp.concatenate(pieces, axis=0)
    from_far = far ^ (row_id // (block_rows * NEAR))
    origin = from_far * NEAR + (me % NEAR ^ (row_id // block_rows % NEAR))
    ordered = jnp.arange(HEAD_SIZE, dtype=i32)[:, None] == (origin * comps + comp_id)[None, :]
    order_k = (ordered & (is_value == 0)[None, :]).astype(bf16)
    order_v = (ordered & (is_value == 1)[None, :]).astype(bf16)
    heads = run(
        attention_kernel,
        "attention",
        shape((count, heads_here * HEAD_SIZE)),
        [VMEM] * 8 + [ANY],
        raw_q,
        raw_kv,
        order_k,
        order_v,
        cos_row,
        sin_row,
        cosine.T,
        sine.T,
        done,
        limit=kernel_mib,
    )

    cuts = ATTN_CUTS
    attn_near = [
        near_scatter(column_blocks(near_arr, heads, (output_w,), cuts, cut, "attn_out")).astype(bf16) for cut in range(cuts)
    ]
    attn_parts = [far_sum(part, far_size) for part in attn_near]
    mixed_parts = [
        (rows.astype(f32) + part).astype(bf16) for rows, part in zip(cut_cols(rows_quarter, cuts), attn_parts)
    ]
    attn_quarter = jnp.concatenate(attn_parts, axis=1).astype(bf16)
    units = gate_weight.shape[1]
    rows_scratch = pltpu.VMEM((count, width // cuts), bf16)
    weights = (near_arr, ffn_gain, in_vmem(gate_w), in_vmem(up_w))
    specs = [SMEM] + [VMEM] * (3 + NEAR)
    first_blocks, last_blocks = (near_gather([part]) for part in mixed_parts)
    *sums, down_a = run(
        functools.partial(hidden_part_kernel, cuts, 0),
        "hidden_part",
        [shape((count, units), f32)] * 2 + [shape((count, 128), f32), pltpu.VMEM((down_half, width), bf16)],
        specs + [HBM],
        *weights,
        *first_blocks,
        pltpu.with_memory_space_constraint(down_weight, pltpu.HBM),
        scratch=[rows_scratch, pltpu.SemaphoreType.DMA],
        limit=kernel_mib,
    )
    kernel = functools.partial(hidden_kernel, cuts)
    hidden = run(
        kernel,
        "hidden",
        shape((count, units)),
        specs + [VMEM] * len(sums),
        *weights,
        *last_blocks,
        *sums,
        scratch=[rows_scratch],
        limit=kernel_mib,
    )

    cuts = BACK_CUTS
    spread = select.reshape(count, far_size, NEAR * MOST)
    deltas = []
    for cut, attn_part in enumerate(cut_cols(attn_quarter, cuts)):
        blocks = column_blocks(near_arr, hidden, (in_vmem(down_a), in_vmem(down_b)), cuts, cut, "ffn_out")
        ffn_part = near_scatter(blocks).astype(bf16)
        delta = dot_tn(spread[:, 0], ffn_part) + dot_tn(spread[:, 0], attn_part)
        for k in range(1, far_size):
            delta = delta + swap(dot_tn(spread[:, k], ffn_part).astype(bf16), far_mask(k)).astype(f32)
        deltas.append(delta.astype(bf16))
    delta = jnp.concatenate(deltas, axis=1).reshape(NEAR, MOST, quarter)
    back = [delta[0]] + [swap(delta[k], k) for k in (1, 2, 3)]
    return pl.pallas_call(
        put_kernel,
        in_specs=[SMEM] + [VMEM] * (3 + NEAR),
        out_specs=HBM,
        out_shape=shape((tok_local, width)),
        scratch_shapes=[pltpu.VMEM((tok_local, width), bf16), pltpu.SemaphoreType.DMA((NEAR,))],
        compiler_params=pltpu.CompilerParams(vmem_limit_bytes=4 * MIB),
        name="put",
    )(near_arr, flags_row, gate_scales.reshape(1, tok_local), tokens, *back)


def solution(mesh):
    in_specs = (
        P(("dp", "ctx"), None),
        P(("dp", "ctx")),
        P(("dp", "ctx")),
        P(),
        P(None, "ctx"),
        P(None, "ctx"),
        P(None, "ctx"),
        P("ctx", None),
        P(),
        P(None, "ctx"),
        P(None, "ctx"),
        P("ctx", None),
    )
    out_specs = P(("dp", "ctx"), None)
    return jax.shard_map(body, mesh=mesh, in_specs=in_specs, out_specs=out_specs, check_vma=False)
```

```python
import functools

import jax
import jax.numpy as jnp
from jax import lax
from jax.experimental import pallas as pl
from jax.experimental.pallas import tpu as pltpu
from jax.sharding import PartitionSpec as P

QUERY_HEADS = 32
KEY_VALUE_HEADS = 8
HEAD_SIZE = 128
PICK_DEV = 16
MOST = 32
NEAR = 4
META = 128
INDEX_ROWS = 16
PICK_ORDER = (1, 2, 3)
ROWS_ORDER = (1, 2, 3)
KEYS_ORDER = (1, 2, 3)
ATTN_ORDER = (3, 1, 2)
MIXED_ORDER = (1, 2, 3)
FFN_ORDER = (3, 1, 2)
BACK_ORDER = (1, 2, 3)
FRONT_CUTS = 2
ATTN_CUTS = 2

norm_eps = 1e-05
rope_base = 500000.0

f32 = jnp.float32
bf16 = jnp.bfloat16
i32 = jnp.int32

VMEM = pl.BlockSpec(memory_space=pltpu.VMEM)
SMEM = pl.BlockSpec(memory_space=pltpu.SMEM)
ANY = pl.BlockSpec(memory_space=pl.ANY)
HBM = pl.BlockSpec(memory_space=pltpu.HBM)
MIB = 1024 * 1024


def swap(value, mask):
    size = lax.axis_size("ctx")
    return lax.ppermute(value, "ctx", [(i, i ^ mask) for i in range(size)])


def far_mask(k):
    return NEAR * k ^ (k & 1) * 2


def quarter_of(device):
    return (device & 3) ^ ((device // NEAR & 1) * 2)


def dot(a, b):
    return jnp.dot(a, b, preferred_element_type=f32)


def dot_nt(a, b):
    return lax.dot_general(a, b, (((1,), (1,)), ((), ())), preferred_element_type=f32)


def dot_tn(a, b):
    return lax.dot_general(a, b, (((0,), (0,)), ((), ())), preferred_element_type=f32)


def span(index, width):
    return pl.ds(pl.multiple_of(index * width, width), width)


def shape(dims, dtype=bf16):
    return jax.ShapeDtypeStruct(dims, dtype)


def run(kernel, name, out_shape, specs, *args, scratch=(), limit=4):
    outs = jax.tree.map(lambda _: VMEM, out_shape)
    return pl.pallas_call(
        kernel,
        in_specs=specs,
        out_specs=outs,
        out_shape=out_shape,
        scratch_shapes=scratch,
        compiler_params=pltpu.CompilerParams(vmem_limit_bytes=limit * MIB),
        name=name,
    )(*args)


def load(weights, after, name, rows=None, zeros=(8, 128)):
    groups = [weight if isinstance(weight, tuple) else (weight,) for weight in weights]
    flat = [weight for group in groups for weight in group]

    def kernel(*refs):
        sources, targets, done, sems = refs[: len(flat)], refs[len(flat) + 1 : -2], refs[-2], refs[-1]
        pairs = []
        for group, target in zip(groups, targets):
            start = 0
            for weight in group:
                source, size = sources[len(pairs)], weight.shape[1]
                pairs.append(
                    (
                        source.at[pl.ds(*rows)] if rows else source,
                        target.at[:, pl.ds(start, size)] if len(group) > 1 else target,
                    )
                )
                start += size
        copies = [pltpu.make_async_copy(source, target, sems.at[i]) for i, (source, target) in enumerate(pairs)]
        for copy in copies:
            copy.start()
        for copy in copies:
            copy.wait()
        done[...] = jnp.zeros_like(done)

    return pl.pallas_call(
        kernel,
        in_specs=[HBM] * len(flat) + [ANY],
        out_specs=[VMEM] * (len(groups) + 1),
        out_shape=[
            pltpu.VMEM((rows[1] if rows else group[0].shape[0], sum(w.shape[1] for w in group)), group[0].dtype)
            for group in groups
        ]
        + [pltpu.VMEM(zeros, i32)],
        scratch_shapes=[pltpu.SemaphoreType.DMA((len(flat),))],
        compiler_params=pltpu.CompilerParams(vmem_limit_bytes=MIB),
        name=name,
    )(*[pltpu.with_memory_space_constraint(w, pltpu.HBM) for w in flat], after)


def in_vmem(value):
    return pltpu.with_memory_space_constraint(value, pltpu.VMEM)


def slots_of(flags):
    tokens = flags.shape[1]
    flag = jnp.broadcast_to(flags.astype(f32), (MOST, tokens))
    upto = lax.broadcasted_iota(i32, (tokens, tokens), 0) <= lax.broadcasted_iota(i32, (tokens, tokens), 1)
    place = dot(flag.astype(bf16), upto.astype(f32).astype(bf16))
    slot = lax.broadcasted_iota(i32, (MOST, tokens), 0).astype(f32) + 1.0
    return jnp.where((place == slot) & (flag > 0.5), 1.0, 0.0)


def pick_kernel(near, flags_hbm, tokens_hbm, *refs):
    outs, (flags, tokens, sems) = refs[:NEAR], refs[NEAR:]
    copies = [
        pltpu.make_async_copy(flags_hbm, flags, sems.at[0]),
        pltpu.make_async_copy(tokens_hbm, tokens, sems.at[1]),
    ]
    for copy in copies:
        copy.start()
    copies[0].wait()
    hot = slots_of(flags[...])
    number = lax.broadcasted_iota(i32, hot.shape, 1).astype(f32) + 1.0
    index = jnp.sum(hot * number, axis=1, keepdims=True) - 1.0
    meta = jnp.broadcast_to(index, (MOST, META)).astype(bf16)
    hot = hot.astype(bf16)
    copies[1].wait()
    for k in range(NEAR):
        width = outs[k].shape[1] - META
        outs[k][:, META:] = dot(hot, tokens[:, span(near[0] ^ k, width)]).astype(bf16)
        outs[k][:, :META] = meta


def pack_kernel(start, wide, done, *refs):
    blocks, out = refs[:NEAR], refs[NEAR]
    for k, block in enumerate(blocks):
        out[k * MOST : (k + 1) * MOST] = block[:, start : start + wide]
    slots = NEAR * MOST
    if out.shape[0] > slots:
        index = jnp.concatenate([block[:, :slots].astype(f32) for block in blocks], axis=0)
        corner = lax.broadcasted_iota(i32, (slots, slots), 0) == lax.broadcasted_iota(i32, (slots, slots), 1)
        row = jnp.sum(jnp.where(corner, index, 0.0), axis=0, keepdims=True)
        out[slots:] = jnp.zeros((INDEX_ROWS, wide), bf16)
        out[slots:, :slots] = jnp.broadcast_to(row, (INDEX_ROWS, slots)).astype(bf16)


def put_kernel(near, flags, scales, tokens, *refs):
    blocks, (out, held, sems) = refs[:NEAR], refs[NEAR:]
    hot = (slots_of(flags[...]) * scales[...].astype(f32)).astype(bf16)
    copies = []
    for k, block in enumerate(blocks):
        cols = span(near[0] ^ k, block.shape[1])
        held[:, cols] = (tokens[:, cols].astype(f32) + dot_tn(hot, block[...])).astype(bf16)
        copies.append(pltpu.make_async_copy(held.at[:, cols], out.at[:, cols], sems.at[k]))
        copies[-1].start()
    for copy in copies:
        copy.wait()


def part_cols(near, index, cuts, width):
    return span((near[0] ^ index // cuts) * cuts + index % cuts, width)


def normed(near, blocks, gain, out):
    width = out.shape[1]
    total = 0.0
    for block in blocks:
        value = block[...].astype(f32)
        total += jnp.sum(value * value, axis=1, keepdims=True)
    scale = lax.rsqrt(total * (1.0 / width) + norm_eps)
    for i, block in enumerate(blocks):
        cols = part_cols(near, i, len(blocks) // NEAR, block.shape[1])
        out[:, cols] = (block[...].astype(f32) * scale * gain[:, cols]).astype(bf16)


def kv_kernel(near, gain, kv_weight, place, done, *refs):
    blocks, (rows, *outs) = refs[: -1 - NEAR], refs[-1 - NEAR :]
    normed(near, blocks, gain, rows)
    both = dot(rows[...], kv_weight[...]).astype(bf16)
    sends = dot_nt(place[...], both).astype(bf16)
    height = outs[0].shape[0]
    for k, out in enumerate(outs):
        out[...] = sends[k * height : (k + 1) * height]


def matmul_kernel(left, right, out):
    out[...] = dot(left[...], right[...]).astype(out.dtype)


def attention_kernel(raw_q, raw_kv, order_k, order_v, cos_row, sin_row, cos_col, sin_col, done, out):
    half = HEAD_SIZE // 2
    keys = dot(order_k[...], raw_kv[...])
    values = dot(order_v[...], raw_kv[...]).astype(bf16)
    low, high = keys[:half], keys[half:]
    cosine, sine = cos_col[...], sin_col[...]
    keys = jnp.concatenate((low * cosine - high * sine, high * cosine + low * sine), axis=0).astype(bf16)
    count = raw_q.shape[0]
    allowed = lax.broadcasted_iota(i32, (count, count), 1) <= lax.broadcasted_iota(i32, (count, count), 0)
    for head in range(raw_q.shape[1] // HEAD_SIZE):
        cols = slice(head * HEAD_SIZE, (head + 1) * HEAD_SIZE)
        query = raw_q[:, cols]
        query = (query * cos_row[...] + pltpu.roll(query, half, 1) * sin_row[...]).astype(bf16)
        scores = dot(query, keys) * (1.0 / HEAD_SIZE**0.5)
        scores = jnp.where(allowed, scores, -jnp.inf)
        terms = jnp.exp(scores - jnp.max(scores, axis=1, keepdims=True))
        probs = (terms / jnp.sum(terms, axis=1, keepdims=True)).astype(bf16)
        out[:, cols] = dot_nt(probs, values).astype(bf16)


def block_kernel(start, near, left, *refs):
    rights, outs = refs[:-NEAR], refs[-NEAR:]
    depth, quarter, wide = rights[0].shape[0], rights[0].shape[1] // NEAR, outs[0].shape[1]
    for k in (3, 1, 2, 0):
        cols = pl.ds(pl.multiple_of((near[0] ^ k) * quarter + start, 128), wide)
        total = 0.0
        for i, right in enumerate(rights):
            total += dot(left[:, i * depth : (i + 1) * depth], right[:, cols])
        outs[k][...] = total.astype(bf16)


def gained(near, blocks, gain, out, cuts, cut):
    total = 0.0
    for k, block in enumerate(blocks):
        width = block.shape[1]
        value = block[...].astype(f32)
        total += jnp.sum(value * value, axis=1, keepdims=True)
        out[:, k * width : (k + 1) * width] = (value * gain[:, part_cols(near, k * cuts + cut, cuts, width)]).astype(bf16)
    return total


def cut_dot(near, rows, weight, cuts, cut):
    width = rows.shape[1] // NEAR
    total = 0.0
    for k in range(NEAR):
        depth = part_cols(near, k * cuts + cut, cuts, width)
        total += dot(rows[:, k * width : (k + 1) * width], weight[depth, :])
    return total


def hidden_part_kernel(cuts, cut, near, gain, gate, up, *refs):
    blocks, (down, gate_sum, up_sum, square_sum, down_first, rows, sem) = refs[:NEAR], refs[NEAR:]
    copy = pltpu.make_async_copy(down.at[pl.ds(0, down_first.shape[0])], down_first, sem)
    copy.start()
    total = gained(near, blocks, gain, rows, cuts, cut)
    square_sum[...] = jnp.broadcast_to(total, square_sum.shape)
    gate_sum[...] = cut_dot(near, rows, gate, cuts, cut)
    up_sum[...] = cut_dot(near, rows, up, cuts, cut)
    copy.wait()


def hidden_kernel(cuts, near, gain, gate, up, *refs):
    blocks, sums, (out, rows) = refs[:NEAR], refs[NEAR:-2], refs[-2:]
    total = gained(near, blocks, gain, rows, cuts, cuts - 1)
    gate_sum = cut_dot(near, rows, gate, cuts, cuts - 1)
    up_sum = cut_dot(near, rows, up, cuts, cuts - 1)
    for gate_part, up_part, square_part in zip(sums[::3], sums[1::3], sums[2::3]):
        gate_sum += gate_part[...]
        up_sum += up_part[...]
        total += square_part[:, :1]
    scale = lax.rsqrt(total * (1.0 / gate.shape[0]) + norm_eps)
    out[...] = (jax.nn.silu(gate_sum * scale) * (up_sum * scale)).astype(bf16)


def column_blocks(near_arr, left, rights, start, wide, name):
    kernel = functools.partial(block_kernel, start)
    outs = [shape((left.shape[0], wide))] * NEAR
    return run(kernel, name, outs, [SMEM, VMEM] + [VMEM] * len(rights), near_arr, left, *rights)


def near_swap(blocks, order):
    got = {0: blocks[0]}
    for k in order:
        got[k] = swap(blocks[k], k)
    return [got[k] for k in range(NEAR)]


def near_gather(parts, order):
    got = [near_swap([part] * NEAR, order) for part in parts]
    return [cut[k] for k in range(NEAR) for cut in got]


def cut_cols(matrix, cuts):
    width = matrix.shape[1] // cuts
    return [matrix[:, i * width : (i + 1) * width] for i in range(cuts)]


def near_scatter(blocks, order):
    return sum(block.astype(f32) for block in near_swap(blocks, order))


def far_sum(block, far_size):
    sent = block.astype(bf16)
    total = sent.astype(f32)
    for k in range(1, far_size):
        total = total + swap(sent, far_mask(k)).astype(f32)
    return total


def body(
    tokens,
    pick_flags,
    gate_scales,
    attn_gain,
    query_weight,
    key_weight,
    value_matrix,
    output_weight,
    ffn_gain,
    gate_weight,
    up_weight,
    down_weight,
):
    tok_local, width = tokens.shape
    size = lax.axis_size("ctx")
    far_size = size // NEAR
    me = lax.axis_index("ctx")
    far = me // NEAR
    near = quarter_of(me)
    near_arr = near.astype(i32).reshape(1)
    count = PICK_DEV * size
    quarter = width // NEAR
    kernel_mib = 6 if count <= 128 else 24
    flags_row = pick_flags.reshape(1, tok_local)
    attn_gain, ffn_gain = attn_gain.reshape(1, width), ffn_gain.reshape(1, width)

    parts = run(
        pick_kernel,
        "pick",
        [shape((MOST, quarter + META))] * NEAR,
        [SMEM, HBM, HBM],
        near_arr,
        pltpu.with_memory_space_constraint(flags_row, pltpu.HBM),
        pltpu.with_memory_space_constraint(tokens, pltpu.HBM),
        scratch=[
            pltpu.VMEM((1, tok_local), i32),
            pltpu.VMEM((tok_local, width), bf16),
            pltpu.SemaphoreType.DMA((2,)),
        ],
    )
    side_by_side = key_weight.shape[1] % 128 == 0
    kv_weights = ((key_weight, value_matrix),) if side_by_side else (key_weight, value_matrix)
    *kv_parts, query_w, output_w, done = load((*kv_weights, query_weight, output_weight), parts[0], "load_qkvo")
    kv_w = kv_parts[0] if side_by_side else jnp.concatenate(kv_parts, axis=1)

    cuts = FRONT_CUTS
    wide = quarter // cuts
    near_parts = near_swap(parts, PICK_ORDER)
    half_slots = NEAR * MOST
    all_rows, index_rows = [], []
    for cut in range(cuts):
        piece = run(
            functools.partial(pack_kernel, META + cut * wide, wide),
            "pack",
            shape((half_slots + (0 if cut else INDEX_ROWS), wide)),
            [ANY] + [VMEM] * NEAR,
            done,
            *near_parts,
        )
        if cut == 0:
            gate_w, done = load((gate_weight,), piece, "load_gate")
        received = [piece] + [swap(piece, far_mask(k)) for k in range(1, far_size)]
        if cut == 0:
            index_rows = [rows[half_slots, :half_slots] for rows in received]
        all_rows.append(jnp.concatenate([rows[:half_slots] for rows in received], axis=0))
    slots = size * MOST
    all_index = jnp.concatenate(index_rows).astype(i32)
    order = jnp.arange(slots, dtype=i32)
    far_of = far ^ (order // (NEAR * MOST))
    device_of = far_of * NEAR + (near ^ (order // MOST % NEAR) ^ (far_of & 1) * 2)
    taken = (all_index >= 0).astype(f32)
    earlier = (device_of[:, None] < device_of[None, :]).astype(f32)
    rank_of = jnp.sum(earlier * taken[:, None], axis=0).astype(i32) + order % MOST
    pick_ids = jnp.arange(count, dtype=i32)
    select = (pick_ids[:, None] == rank_of[None, :]) & (all_index >= 0)[None, :]
    token_positions = jnp.sum(jnp.where(select, (device_of * tok_local + all_index)[None, :], 0), axis=1)
    select = select.astype(bf16)
    row_parts = [dot(select, piece).astype(bf16) for piece in all_rows]
    up_w, done = load((up_weight,), row_parts[0], "load_up")
    row_blocks = near_gather(row_parts, ROWS_ORDER)
    rows_quarter = jnp.concatenate(row_parts, axis=1)

    half_dim = HEAD_SIZE // 2
    frequency = rope_base ** (-(jnp.arange(half_dim, dtype=f32) * 2.0) / HEAD_SIZE)
    angles = token_positions.astype(f32)[:, None] * frequency[None, :]
    cosine, sine = jnp.cos(angles), jnp.sin(angles)
    cos_row = jnp.concatenate((cosine, cosine), axis=1)
    sin_row = jnp.concatenate((-sine, sine), axis=1)

    comps = key_weight.shape[1] // KEY_VALUE_HEADS
    heads_here = query_weight.shape[1] // HEAD_SIZE
    group_width = QUERY_HEADS // KEY_VALUE_HEADS
    block_rows = 2 * comps
    total_rows = size * block_rows
    row_id = jnp.arange(total_rows, dtype=i32)
    comp_id, is_value = row_id % comps, row_id // comps % 2
    to_far = far ^ (row_id // block_rows % far_size)
    target = to_far * NEAR + (me % NEAR ^ (row_id // (block_rows * far_size)))
    column = comp_id * KEY_VALUE_HEADS + target * heads_here // group_width
    col_id = jnp.arange(key_weight.shape[1], dtype=i32)
    place = column[:, None] == col_id[None, :]
    place = jnp.concatenate([place & (is_value == part)[:, None] for part in (0, 1)], axis=1).astype(bf16)
    rows_normed, *sends = run(
        kv_kernel,
        "keys_values",
        [shape((count, width))] + [shape((total_rows // NEAR, count))] * NEAR,
        [SMEM] + [VMEM] * 3 + [ANY] + [VMEM] * len(row_blocks),
        near_arr,
        attn_gain,
        kv_w,
        place,
        done,
        *row_blocks,
        limit=kernel_mib,
    )
    down_half = down_weight.shape[0] // 2
    got = near_swap(sends, KEYS_ORDER)
    raw_q = run(
        matmul_kernel, "query", shape((count, heads_here * HEAD_SIZE), f32), [VMEM, VMEM], rows_normed, query_w
    )
    pieces = []
    for k in range(far_size):
        piece = jnp.concatenate([g[k * block_rows : (k + 1) * block_rows] for g in got], axis=0)
        pieces.append(swap(piece, NEAR * k) if k else piece)
    down_b, done = load((down_weight,), pieces[0], "load_down", (down_half, down_half))
    raw_kv = jnp.concatenate(pieces, axis=0)
    from_far = far ^ (row_id // (block_rows * NEAR))
    origin = from_far * NEAR + (me % NEAR ^ (row_id // block_rows % NEAR))
    ordered = jnp.arange(HEAD_SIZE, dtype=i32)[:, None] == (origin * comps + comp_id)[None, :]
    order_k = (ordered & (is_value == 0)[None, :]).astype(bf16)
    order_v = (ordered & (is_value == 1)[None, :]).astype(bf16)
    heads = run(
        attention_kernel,
        "attention",
        shape((count, heads_here * HEAD_SIZE)),
        [VMEM] * 8 + [ANY],
        raw_q,
        raw_kv,
        order_k,
        order_v,
        cos_row,
        sin_row,
        cosine.T,
        sine.T,
        done,
        limit=kernel_mib,
    )

    cuts = ATTN_CUTS
    attn_near = [
        near_scatter(column_blocks(near_arr, heads, (output_w,), cut * (quarter // cuts), quarter // cuts, "attn_out"), ATTN_ORDER).astype(bf16) for cut in range(cuts)
    ]
    attn_parts = [far_sum(part, far_size) for part in attn_near]
    mixed_parts = [
        (rows.astype(f32) + part).astype(bf16) for rows, part in zip(cut_cols(rows_quarter, cuts), attn_parts)
    ]
    units = gate_weight.shape[1]
    rows_scratch = pltpu.VMEM((count, width // cuts), bf16)
    weights = (near_arr, ffn_gain, in_vmem(gate_w), in_vmem(up_w))
    specs = [SMEM] + [VMEM] * (3 + NEAR)
    first_blocks, last_blocks = (near_gather([part], MIXED_ORDER) for part in mixed_parts)
    *sums, down_a = run(
        functools.partial(hidden_part_kernel, cuts, 0),
        "hidden_part",
        [shape((count, units), f32)] * 2 + [shape((count, 128), f32), pltpu.VMEM((down_half, width), bf16)],
        specs + [HBM],
        *weights,
        *first_blocks,
        pltpu.with_memory_space_constraint(down_weight, pltpu.HBM),
        scratch=[rows_scratch, pltpu.SemaphoreType.DMA],
        limit=kernel_mib,
    )
    kernel = functools.partial(hidden_kernel, cuts)
    hidden = run(
        kernel,
        "hidden",
        shape((count, units)),
        specs + [VMEM] * len(sums),
        *weights,
        *last_blocks,
        *sums,
        scratch=[rows_scratch],
        limit=kernel_mib,
    )

    attn_quarter = jnp.concatenate(attn_parts, axis=1).astype(bf16)
    spread = select.reshape(count, far_size, NEAR * MOST)
    deltas = []
    for cut in range(cuts):
        start, stop = cut * (quarter // cuts), (cut + 1) * (quarter // cuts)
        blocks = column_blocks(
            near_arr, hidden, (in_vmem(down_a), in_vmem(down_b)), start, stop - start, "ffn_out"
        )
        ffn_part = near_scatter(blocks, FFN_ORDER).astype(bf16)
        delta = dot_tn(spread[:, 0], ffn_part) + dot_tn(spread[:, 0], attn_quarter[:, start:stop])
        for k in range(1, far_size):
            delta = delta + swap(dot_tn(spread[:, k], ffn_part).astype(bf16), far_mask(k)).astype(f32)
        deltas.append(delta.astype(bf16))
    delta = jnp.concatenate(deltas, axis=1).reshape(NEAR, MOST, quarter)
    back = near_swap(delta, BACK_ORDER)
    return pl.pallas_call(
        put_kernel,
        in_specs=[SMEM] + [VMEM] * (3 + NEAR),
        out_specs=HBM,
        out_shape=shape((tok_local, width)),
        scratch_shapes=[pltpu.VMEM((tok_local, width), bf16), pltpu.SemaphoreType.DMA((NEAR,))],
        compiler_params=pltpu.CompilerParams(vmem_limit_bytes=4 * MIB),
        name="put",
    )(near_arr, flags_row, gate_scales.reshape(1, tok_local), tokens, *back)


def solution(mesh):
    in_specs = (
        P(("dp", "ctx"), None),
        P(("dp", "ctx")),
        P(("dp", "ctx")),
        P(),
        P(None, "ctx"),
        P(None, "ctx"),
        P(None, "ctx"),
        P("ctx", None),
        P(),
        P(None, "ctx"),
        P(None, "ctx"),
        P("ctx", None),
    )
    out_specs = P(("dp", "ctx"), None)
    return jax.shard_map(body, mesh=mesh, in_specs=in_specs, out_specs=out_specs, check_vma=False)
```

```python
import functools

import jax
import jax.numpy as jnp
from jax import lax
from jax.experimental import pallas as pl
from jax.experimental.pallas import tpu as pltpu
from jax.sharding import PartitionSpec as P

QUERY_HEADS = 32
KEY_VALUE_HEADS = 8
HEAD_SIZE = 128
PICK_DEV = 16
MOST = 32
NEAR = 4
META = 128
INDEX_ROWS = 16
PICK_ORDER = (1, 2, 3)
ROWS_ORDER = (1, 2, 3)
KEYS_ORDER = (1, 2, 3)
ATTN_ORDER = (3, 1, 2)
MIXED_ORDER = (1, 2, 3)
FFN_ORDER = (3, 1, 2)
BACK_ORDER = (1, 2, 3)
FRONT_CUTS = 2
ATTN_CUTS = 2

norm_eps = 1e-05
rope_base = 500000.0

f32 = jnp.float32
bf16 = jnp.bfloat16
i32 = jnp.int32

VMEM = pl.BlockSpec(memory_space=pltpu.VMEM)
SMEM = pl.BlockSpec(memory_space=pltpu.SMEM)
ANY = pl.BlockSpec(memory_space=pl.ANY)
HBM = pl.BlockSpec(memory_space=pltpu.HBM)
MIB = 1024 * 1024


def swap(value, mask):
    size = lax.axis_size("ctx")
    return lax.ppermute(value, "ctx", [(i, i ^ mask) for i in range(size)])


def far_mask(k):
    return NEAR * k ^ (k & 1) * 2


def quarter_of(device):
    return (device & 3) ^ ((device // NEAR & 1) * 2)


def dot(a, b):
    return jnp.dot(a, b, preferred_element_type=f32)


def dot_nt(a, b):
    return lax.dot_general(a, b, (((1,), (1,)), ((), ())), preferred_element_type=f32)


def dot_tn(a, b):
    return lax.dot_general(a, b, (((0,), (0,)), ((), ())), preferred_element_type=f32)


def span(index, width):
    return pl.ds(pl.multiple_of(index * width, width), width)


def shape(dims, dtype=bf16):
    return jax.ShapeDtypeStruct(dims, dtype)


def run(kernel, name, out_shape, specs, *args, scratch=(), limit=4):
    outs = jax.tree.map(lambda _: VMEM, out_shape)
    return pl.pallas_call(
        kernel,
        in_specs=specs,
        out_specs=outs,
        out_shape=out_shape,
        scratch_shapes=scratch,
        compiler_params=pltpu.CompilerParams(vmem_limit_bytes=limit * MIB),
        name=name,
    )(*args)


def load(weights, after, name, rows=None, zeros=(8, 128)):
    groups = [weight if isinstance(weight, tuple) else (weight,) for weight in weights]
    flat = [weight for group in groups for weight in group]

    def kernel(*refs):
        sources, targets, done, sems = refs[: len(flat)], refs[len(flat) + 1 : -2], refs[-2], refs[-1]
        pairs = []
        for group, target in zip(groups, targets):
            start = 0
            for weight in group:
                source, size = sources[len(pairs)], weight.shape[1]
                pairs.append(
                    (
                        source.at[pl.ds(*rows)] if rows else source,
                        target.at[:, pl.ds(start, size)] if len(group) > 1 else target,
                    )
                )
                start += size
        copies = [pltpu.make_async_copy(source, target, sems.at[i]) for i, (source, target) in enumerate(pairs)]
        for copy in copies:
            copy.start()
        for copy in copies:
            copy.wait()
        done[...] = jnp.zeros_like(done)

    return pl.pallas_call(
        kernel,
        in_specs=[HBM] * len(flat) + [ANY],
        out_specs=[VMEM] * (len(groups) + 1),
        out_shape=[
            pltpu.VMEM((rows[1] if rows else group[0].shape[0], sum(w.shape[1] for w in group)), group[0].dtype)
            for group in groups
        ]
        + [pltpu.VMEM(zeros, i32)],
        scratch_shapes=[pltpu.SemaphoreType.DMA((len(flat),))],
        compiler_params=pltpu.CompilerParams(vmem_limit_bytes=MIB),
        name=name,
    )(*[pltpu.with_memory_space_constraint(w, pltpu.HBM) for w in flat], after)


def in_vmem(value):
    return pltpu.with_memory_space_constraint(value, pltpu.VMEM)


def slots_of(flags):
    tokens = flags.shape[1]
    flag = jnp.broadcast_to(flags.astype(f32), (MOST, tokens))
    upto = lax.broadcasted_iota(i32, (tokens, tokens), 0) <= lax.broadcasted_iota(i32, (tokens, tokens), 1)
    place = dot(flag.astype(bf16), upto.astype(f32).astype(bf16))
    slot = lax.broadcasted_iota(i32, (MOST, tokens), 0).astype(f32) + 1.0
    return jnp.where((place == slot) & (flag > 0.5), 1.0, 0.0)


def pick_kernel(near, flags_hbm, tokens_hbm, *refs):
    outs, (flags, tokens, sems) = refs[:NEAR], refs[NEAR:]
    copies = [
        pltpu.make_async_copy(flags_hbm, flags, sems.at[0]),
        pltpu.make_async_copy(tokens_hbm, tokens, sems.at[1]),
    ]
    for copy in copies:
        copy.start()
    copies[0].wait()
    hot = slots_of(flags[...])
    number = lax.broadcasted_iota(i32, hot.shape, 1).astype(f32) + 1.0
    index = jnp.sum(hot * number, axis=1, keepdims=True) - 1.0
    meta = jnp.broadcast_to(index, (MOST, META)).astype(bf16)
    hot = hot.astype(bf16)
    copies[1].wait()
    for k in range(NEAR):
        width = outs[k].shape[1] - META
        outs[k][:, META:] = dot(hot, tokens[:, span(near[0] ^ k, width)]).astype(bf16)
        outs[k][:, :META] = meta


def pack_kernel(start, wide, done, *refs):
    blocks, out = refs[:NEAR], refs[NEAR]
    for k, block in enumerate(blocks):
        out[k * MOST : (k + 1) * MOST] = block[:, start : start + wide]
    slots = NEAR * MOST
    if out.shape[0] > slots:
        index = jnp.concatenate([block[:, :slots].astype(f32) for block in blocks], axis=0)
        corner = lax.broadcasted_iota(i32, (slots, slots), 0) == lax.broadcasted_iota(i32, (slots, slots), 1)
        row = jnp.sum(jnp.where(corner, index, 0.0), axis=0, keepdims=True)
        out[slots:] = jnp.zeros((INDEX_ROWS, wide), bf16)
        out[slots:, :slots] = jnp.broadcast_to(row, (INDEX_ROWS, slots)).astype(bf16)


def put_kernel(near, flags, scales, tokens, *refs):
    blocks, (out, held, sems) = refs[:NEAR], refs[NEAR:]
    hot = (slots_of(flags[...]) * scales[...].astype(f32)).astype(bf16)
    copies = []
    for k, block in enumerate(blocks):
        cols = span(near[0] ^ k, block.shape[1])
        held[:, cols] = (tokens[:, cols].astype(f32) + dot_tn(hot, block[...])).astype(bf16)
        copies.append(pltpu.make_async_copy(held.at[:, cols], out.at[:, cols], sems.at[k]))
        copies[-1].start()
    for copy in copies:
        copy.wait()


def part_cols(near, index, cuts, width):
    return span((near[0] ^ index // cuts) * cuts + index % cuts, width)


def normed(near, blocks, gain, out):
    width = out.shape[1]
    total = 0.0
    for block in blocks:
        value = block[...].astype(f32)
        total += jnp.sum(value * value, axis=1, keepdims=True)
    scale = lax.rsqrt(total * (1.0 / width) + norm_eps)
    for i, block in enumerate(blocks):
        cols = part_cols(near, i, len(blocks) // NEAR, block.shape[1])
        out[:, cols] = (block[...].astype(f32) * scale * gain[:, cols]).astype(bf16)


def kv_kernel(near, gain, kv_weight, place, done, *refs):
    blocks, (rows, *outs) = refs[: -1 - NEAR], refs[-1 - NEAR :]
    normed(near, blocks, gain, rows)
    both = dot(rows[...], kv_weight[...]).astype(bf16)
    sends = dot_nt(place[...], both).astype(bf16)
    height = outs[0].shape[0]
    for k, out in enumerate(outs):
        out[...] = sends[k * height : (k + 1) * height]


def matmul_kernel(left, right, out):
    out[...] = dot(left[...], right[...]).astype(out.dtype)


def attention_kernel(raw_q, raw_kv, order_k, order_v, cos_row, sin_row, cos_col, sin_col, done, out):
    half = HEAD_SIZE // 2
    keys = dot(order_k[...], raw_kv[...])
    values = dot(order_v[...], raw_kv[...]).astype(bf16)
    low, high = keys[:half], keys[half:]
    cosine, sine = cos_col[...], sin_col[...]
    keys = jnp.concatenate((low * cosine - high * sine, high * cosine + low * sine), axis=0).astype(bf16)
    count = raw_q.shape[0]
    allowed = lax.broadcasted_iota(i32, (count, count), 1) <= lax.broadcasted_iota(i32, (count, count), 0)
    for head in range(raw_q.shape[1] // HEAD_SIZE):
        cols = slice(head * HEAD_SIZE, (head + 1) * HEAD_SIZE)
        query = raw_q[:, cols]
        query = (query * cos_row[...] + pltpu.roll(query, half, 1) * sin_row[...]).astype(bf16)
        scores = dot(query, keys) * (1.0 / HEAD_SIZE**0.5)
        scores = jnp.where(allowed, scores, -jnp.inf)
        terms = jnp.exp(scores - jnp.max(scores, axis=1, keepdims=True))
        probs = (terms / jnp.sum(terms, axis=1, keepdims=True)).astype(bf16)
        out[:, cols] = dot_nt(probs, values).astype(bf16)


def block_kernel(start, near, left, *refs):
    rights, outs = refs[:-NEAR], refs[-NEAR:]
    depth, quarter, wide = rights[0].shape[0], rights[0].shape[1] // NEAR, outs[0].shape[1]
    for k in (3, 1, 2, 0):
        cols = pl.ds(pl.multiple_of((near[0] ^ k) * quarter + start, 128), wide)
        total = 0.0
        for i, right in enumerate(rights):
            total += dot(left[:, i * depth : (i + 1) * depth], right[:, cols])
        outs[k][...] = total.astype(bf16)


def gained(near, blocks, gain, out, cuts, cut):
    total = 0.0
    for k, block in enumerate(blocks):
        width = block.shape[1]
        value = block[...].astype(f32)
        total += jnp.sum(value * value, axis=1, keepdims=True)
        out[:, k * width : (k + 1) * width] = (value * gain[:, part_cols(near, k * cuts + cut, cuts, width)]).astype(bf16)
    return total


def cut_dot(near, rows, weight, cuts, cut):
    width = rows.shape[1] // NEAR
    total = 0.0
    for k in range(NEAR):
        depth = part_cols(near, k * cuts + cut, cuts, width)
        total += dot(rows[:, k * width : (k + 1) * width], weight[depth, :])
    return total


def hidden_part_kernel(cuts, cut, near, gain, gate, up, *refs):
    blocks, (down, gate_sum, up_sum, square_sum, down_first, rows, sem) = refs[:NEAR], refs[NEAR:]
    copy = pltpu.make_async_copy(down.at[pl.ds(0, down_first.shape[0])], down_first, sem)
    copy.start()
    total = gained(near, blocks, gain, rows, cuts, cut)
    square_sum[...] = jnp.broadcast_to(total, square_sum.shape)
    gate_sum[...] = cut_dot(near, rows, gate, cuts, cut)
    up_sum[...] = cut_dot(near, rows, up, cuts, cut)
    copy.wait()


def hidden_kernel(cuts, near, gain, gate, up, *refs):
    blocks, sums, (out, rows) = refs[:NEAR], refs[NEAR:-2], refs[-2:]
    total = gained(near, blocks, gain, rows, cuts, cuts - 1)
    gate_sum = cut_dot(near, rows, gate, cuts, cuts - 1)
    up_sum = cut_dot(near, rows, up, cuts, cuts - 1)
    for gate_part, up_part, square_part in zip(sums[::3], sums[1::3], sums[2::3]):
        gate_sum += gate_part[...]
        up_sum += up_part[...]
        total += square_part[:, :1]
    scale = lax.rsqrt(total * (1.0 / gate.shape[0]) + norm_eps)
    out[...] = (jax.nn.silu(gate_sum * scale) * (up_sum * scale)).astype(bf16)


def column_blocks(near_arr, left, rights, start, wide, name):
    kernel = functools.partial(block_kernel, start)
    outs = [shape((left.shape[0], wide))] * NEAR
    return run(kernel, name, outs, [SMEM, VMEM] + [VMEM] * len(rights), near_arr, left, *rights)


def near_swap(blocks, order):
    got = {0: blocks[0]}
    for k in order:
        got[k] = swap(blocks[k], k)
    return [got[k] for k in range(NEAR)]


def near_gather(parts, order):
    got = [near_swap([part] * NEAR, order) for part in parts]
    return [cut[k] for k in range(NEAR) for cut in got]


def cut_cols(matrix, cuts):
    width = matrix.shape[1] // cuts
    return [matrix[:, i * width : (i + 1) * width] for i in range(cuts)]


def near_scatter(blocks, order):
    return sum(block.astype(f32) for block in near_swap(blocks, order))


def far_sum(block, far_size):
    sent = block.astype(bf16)
    total = sent.astype(f32)
    for k in range(1, far_size):
        total = total + swap(sent, far_mask(k)).astype(f32)
    return total


def body(
    tokens,
    pick_flags,
    gate_scales,
    attn_gain,
    query_weight,
    key_weight,
    value_matrix,
    output_weight,
    ffn_gain,
    gate_weight,
    up_weight,
    down_weight,
):
    tok_local, width = tokens.shape
    size = lax.axis_size("ctx")
    far_size = size // NEAR
    me = lax.axis_index("ctx")
    far = me // NEAR
    near = quarter_of(me)
    near_arr = near.astype(i32).reshape(1)
    count = PICK_DEV * size
    quarter = width // NEAR
    kernel_mib = 6 if count <= 128 else 24
    flags_row = pick_flags.reshape(1, tok_local)
    attn_gain, ffn_gain = attn_gain.reshape(1, width), ffn_gain.reshape(1, width)

    parts = run(
        pick_kernel,
        "pick",
        [shape((MOST, quarter + META))] * NEAR,
        [SMEM, HBM, HBM],
        near_arr,
        pltpu.with_memory_space_constraint(flags_row, pltpu.HBM),
        pltpu.with_memory_space_constraint(tokens, pltpu.HBM),
        scratch=[
            pltpu.VMEM((1, tok_local), i32),
            pltpu.VMEM((tok_local, width), bf16),
            pltpu.SemaphoreType.DMA((2,)),
        ],
    )
    side_by_side = key_weight.shape[1] % 128 == 0
    kv_weights = ((key_weight, value_matrix),) if side_by_side else (key_weight, value_matrix)
    *kv_parts, output_w, done = load((*kv_weights, output_weight), parts[0], "load_kvo")
    kv_w = kv_parts[0] if side_by_side else jnp.concatenate(kv_parts, axis=1)

    cuts = FRONT_CUTS
    wide = quarter // cuts
    near_parts = near_swap(parts, PICK_ORDER)
    half_slots = NEAR * MOST
    all_rows, index_rows = [], []
    for cut in range(cuts):
        piece = run(
            functools.partial(pack_kernel, META + cut * wide, wide),
            "pack",
            shape((half_slots + (0 if cut else INDEX_ROWS), wide)),
            [ANY] + [VMEM] * NEAR,
            done,
            *near_parts,
        )
        if cut == 0:
            gate_w, done = load((gate_weight,), piece, "load_gate")
        received = [piece] + [swap(piece, far_mask(k)) for k in range(1, far_size)]
        if cut == 0:
            index_rows = [rows[half_slots, :half_slots] for rows in received]
        all_rows.append(jnp.concatenate([rows[:half_slots] for rows in received], axis=0))
    slots = size * MOST
    all_index = jnp.concatenate(index_rows).astype(i32)
    order = jnp.arange(slots, dtype=i32)
    far_of = far ^ (order // (NEAR * MOST))
    device_of = far_of * NEAR + (near ^ (order // MOST % NEAR) ^ (far_of & 1) * 2)
    taken = (all_index >= 0).astype(f32)
    earlier = (device_of[:, None] < device_of[None, :]).astype(f32)
    rank_of = jnp.sum(earlier * taken[:, None], axis=0).astype(i32) + order % MOST
    pick_ids = jnp.arange(count, dtype=i32)
    select = (pick_ids[:, None] == rank_of[None, :]) & (all_index >= 0)[None, :]
    token_positions = jnp.sum(jnp.where(select, (device_of * tok_local + all_index)[None, :], 0), axis=1)
    select = select.astype(bf16)
    row_parts = [dot(select, piece).astype(bf16) for piece in all_rows]
    up_w, done = load((up_weight,), row_parts[0], "load_up")
    row_blocks = near_gather(row_parts, ROWS_ORDER)
    rows_quarter = jnp.concatenate(row_parts, axis=1)

    half_dim = HEAD_SIZE // 2
    frequency = rope_base ** (-(jnp.arange(half_dim, dtype=f32) * 2.0) / HEAD_SIZE)
    angles = token_positions.astype(f32)[:, None] * frequency[None, :]
    cosine, sine = jnp.cos(angles), jnp.sin(angles)
    cos_row = jnp.concatenate((cosine, cosine), axis=1)
    sin_row = jnp.concatenate((-sine, sine), axis=1)

    comps = key_weight.shape[1] // KEY_VALUE_HEADS
    heads_here = query_weight.shape[1] // HEAD_SIZE
    group_width = QUERY_HEADS // KEY_VALUE_HEADS
    block_rows = 2 * comps
    total_rows = size * block_rows
    row_id = jnp.arange(total_rows, dtype=i32)
    comp_id, is_value = row_id % comps, row_id // comps % 2
    to_far = far ^ (row_id // block_rows % far_size)
    target = to_far * NEAR + (me % NEAR ^ (row_id // (block_rows * far_size)))
    column = comp_id * KEY_VALUE_HEADS + target * heads_here // group_width
    col_id = jnp.arange(key_weight.shape[1], dtype=i32)
    place = column[:, None] == col_id[None, :]
    place = jnp.concatenate([place & (is_value == part)[:, None] for part in (0, 1)], axis=1).astype(bf16)
    rows_normed, *sends = run(
        kv_kernel,
        "keys_values",
        [shape((count, width))] + [shape((total_rows // NEAR, count))] * NEAR,
        [SMEM] + [VMEM] * 3 + [ANY] + [VMEM] * len(row_blocks),
        near_arr,
        attn_gain,
        kv_w,
        place,
        done,
        *row_blocks,
        limit=kernel_mib,
    )
    down_half = down_weight.shape[0] // 2
    query_w, _ = load((query_weight,), sends[0], "load_query")
    got = near_swap(sends, KEYS_ORDER)
    raw_q = run(
        matmul_kernel, "query", shape((count, heads_here * HEAD_SIZE), f32), [VMEM, VMEM], rows_normed, query_w
    )
    pieces = []
    for k in range(far_size):
        piece = jnp.concatenate([g[k * block_rows : (k + 1) * block_rows] for g in got], axis=0)
        pieces.append(swap(piece, NEAR * k) if k else piece)
    down_b, done = load((down_weight,), pieces[0], "load_down", (down_half, down_half))
    raw_kv = jnp.concatenate(pieces, axis=0)
    from_far = far ^ (row_id // (block_rows * NEAR))
    origin = from_far * NEAR + (me % NEAR ^ (row_id // block_rows % NEAR))
    ordered = jnp.arange(HEAD_SIZE, dtype=i32)[:, None] == (origin * comps + comp_id)[None, :]
    order_k = (ordered & (is_value == 0)[None, :]).astype(bf16)
    order_v = (ordered & (is_value == 1)[None, :]).astype(bf16)
    heads = run(
        attention_kernel,
        "attention",
        shape((count, heads_here * HEAD_SIZE)),
        [VMEM] * 8 + [ANY],
        raw_q,
        raw_kv,
        order_k,
        order_v,
        cos_row,
        sin_row,
        cosine.T,
        sine.T,
        done,
        limit=kernel_mib,
    )

    cuts = ATTN_CUTS
    attn_near = [
        near_scatter(column_blocks(near_arr, heads, (output_w,), cut * (quarter // cuts), quarter // cuts, "attn_out"), ATTN_ORDER).astype(bf16) for cut in range(cuts)
    ]
    attn_parts = [far_sum(part, far_size) for part in attn_near]
    mixed_parts = [
        (rows.astype(f32) + part).astype(bf16) for rows, part in zip(cut_cols(rows_quarter, cuts), attn_parts)
    ]
    units = gate_weight.shape[1]
    rows_scratch = pltpu.VMEM((count, width // cuts), bf16)
    weights = (near_arr, ffn_gain, in_vmem(gate_w), in_vmem(up_w))
    specs = [SMEM] + [VMEM] * (3 + NEAR)
    first_blocks, last_blocks = (near_gather([part], MIXED_ORDER) for part in mixed_parts)
    *sums, down_a = run(
        functools.partial(hidden_part_kernel, cuts, 0),
        "hidden_part",
        [shape((count, units), f32)] * 2 + [shape((count, 128), f32), pltpu.VMEM((down_half, width), bf16)],
        specs + [HBM],
        *weights,
        *first_blocks,
        pltpu.with_memory_space_constraint(down_weight, pltpu.HBM),
        scratch=[rows_scratch, pltpu.SemaphoreType.DMA],
        limit=kernel_mib,
    )
    kernel = functools.partial(hidden_kernel, cuts)
    hidden = run(
        kernel,
        "hidden",
        shape((count, units)),
        specs + [VMEM] * len(sums),
        *weights,
        *last_blocks,
        *sums,
        scratch=[rows_scratch],
        limit=kernel_mib,
    )

    attn_quarter = jnp.concatenate(attn_parts, axis=1).astype(bf16)
    spread = select.reshape(count, far_size, NEAR * MOST)
    deltas = []
    for cut in range(cuts):
        start, stop = cut * (quarter // cuts), (cut + 1) * (quarter // cuts)
        blocks = column_blocks(
            near_arr, hidden, (in_vmem(down_a), in_vmem(down_b)), start, stop - start, "ffn_out"
        )
        ffn_part = near_scatter(blocks, FFN_ORDER).astype(bf16)
        delta = dot_tn(spread[:, 0], ffn_part) + dot_tn(spread[:, 0], attn_quarter[:, start:stop])
        for k in range(1, far_size):
            delta = delta + swap(dot_tn(spread[:, k], ffn_part).astype(bf16), far_mask(k)).astype(f32)
        deltas.append(delta.astype(bf16))
    delta = jnp.concatenate(deltas, axis=1).reshape(NEAR, MOST, quarter)
    back = near_swap(delta, BACK_ORDER)
    return pl.pallas_call(
        put_kernel,
        in_specs=[SMEM] + [VMEM] * (3 + NEAR),
        out_specs=HBM,
        out_shape=shape((tok_local, width)),
        scratch_shapes=[pltpu.VMEM((tok_local, width), bf16), pltpu.SemaphoreType.DMA((NEAR,))],
        compiler_params=pltpu.CompilerParams(vmem_limit_bytes=4 * MIB),
        name="put",
    )(near_arr, flags_row, gate_scales.reshape(1, tok_local), tokens, *back)


def solution(mesh):
    in_specs = (
        P(("dp", "ctx"), None),
        P(("dp", "ctx")),
        P(("dp", "ctx")),
        P(),
        P(None, "ctx"),
        P(None, "ctx"),
        P(None, "ctx"),
        P("ctx", None),
        P(),
        P(None, "ctx"),
        P(None, "ctx"),
        P("ctx", None),
    )
    out_specs = P(("dp", "ctx"), None)
    return jax.shard_map(body, mesh=mesh, in_specs=in_specs, out_specs=out_specs, check_vma=False)
```
